32 devices in a mesh: blk: 8 (over y, x, core), lag: 4 (over z).
Axes of the slice: x: 2, y: 2, z: 4, core: 2. Of those that a mesh axis runs over, the one named last changes fastest.
Arguments:
- raw: float32 [8192, 4096], P(('blk', 'lag')), may hold values from -60 to 60
- mask: int32 [8, 8], replicated, may hold values from 0 to 1, as said below
Outputs:
- stack: float32 [8, 8192], P(None, ('blk', 'lag'))
The draws below stay inside these ranges and needn't reach their ends.
Inputs may be any that keep to these rules, and one draw needn't show every extreme that they name: mask is 0 or 1 and symmetric; it is 0 wherever |I - J| exceeds a limit between 4 and 6.
All inputs are finite; a program needn't handle non-finite values.
Results may differ from the reference program's by a relative error of at most 0.008.
Values may be sent and summed in bfloat16 or wider, within the bound.
A program may use at most 192 MiB of HBM per device.

```python
import math
import jax
import jax.numpy as jnp
from jax import lax

NT = 8192
C = 4096
NB = 2048
K0 = 16
SW = 32
TAPER = 128
LAGS = 8
LAG_STEP = 32
BLOCKS = 8
BLOCK_CH = 512
OFFSETS = 8192


def draw_raw(key, part):
    noise_key, scale_key = jax.random.split(jax.random.fold_in(key, 11), 2)
    scales = jnp.exp(jax.random.uniform(scale_key, (1, C), minval=0.0, maxval=math.log(10.0)))
    noise = jax.random.truncated_normal(noise_key, -6.0, 6.0, (NT, C))
    return (scales * noise).astype(jnp.float32)


def draw_mask(key, part):
    alive_key, limit_key, keep_key = jax.random.split(jax.random.fold_in(key, 7), 3)
    labels = jnp.arange(BLOCKS, dtype=jnp.int32)
    keeper = jax.random.randint(keep_key, (), 0, BLOCKS)
    alive = (jax.random.randint(alive_key, (BLOCKS,), 0, 8) > 0) | (labels == keeper)
    limit = jax.random.randint(limit_key, (), BLOCKS // 2, BLOCKS - 1)
    near = jnp.abs(labels[:, None] - labels[None, :]) <= limit
    return (alive[:, None] & alive[None, :] & near).astype(jnp.int32)


def setup_inputs(seed: int = 0) -> dict:
    key_list = jax.random.split(jax.random.key(seed), 3)
    return {
        "raw": draw_raw(jax.random.fold_in(key_list[2], 71), 0),
        "mask": draw_mask(jax.random.fold_in(key_list[2], 71), 0),
    }


EPS = 1e-06

def taper_weights(first_bin, count):
    position = (first_bin + lax.iota(jnp.int32, count)).astype(jnp.float32)
    edge = jnp.minimum(position, NB - 1 - position)
    curve = 0.5 - 0.5 * jnp.cos(math.pi * (edge + 0.5) / TAPER)
    return jnp.where(edge < TAPER, curve, jnp.ones_like(curve))

def lag_phases(bins):
    number = lax.iota(jnp.int32, LAGS)
    shifts = LAG_STEP * (2 * number + 1 - LAGS) // 2
    return jnp.mod(shifts[:, None] * bins[None, :], NT).astype(jnp.float32) * (2 * math.pi / NT)

def moving_mean(padded):
    window = lax.reduce_window(padded, jnp.zeros((), padded.dtype), lax.add, (1, 2 * SW + 1), (1, 1), 'VALID')
    return window / (2 * SW + 1)

def rotate(own_real, own_imag, cosines, sines):
    real_part = own_real.astype(jnp.float32)[None]
    imag_part = own_imag.astype(jnp.float32)[None]
    rot_real = real_part * cosines[:, None, :] - imag_part * sines[:, None, :]
    rot_imag = real_part * sines[:, None, :] + imag_part * cosines[:, None, :]
    joined = jnp.concatenate([rot_real, rot_imag], axis=2).astype(jnp.bfloat16)
    return joined.reshape(joined.shape[0] * joined.shape[1], joined.shape[2])

def diagonal_sums(product, rows):
    count = product.shape[2]
    padded = jnp.pad(product, ((0, 0), (0, 0), (0, rows)))
    width = count + rows - 1
    flat = padded.reshape(product.shape[0], rows * (count + rows))[:, :rows * width]
    return lax.optimization_barrier(jnp.sum(flat.reshape(product.shape[0], rows, width), axis=1))

def place(total, values, first_col):
    anchor = jnp.zeros((), jnp.int32)
    current = lax.dynamic_slice(total, (anchor, first_col), values.shape)
    return lax.dynamic_update_slice(total, current + values, (anchor, first_col))

def pair_counts(mask, columns):
    blocks = mask.shape[0]
    width = C // blocks
    labels = lax.iota(jnp.int32, blocks)
    apart = labels[None, :] - labels[:, None]
    deltas = lax.iota(jnp.int32, 2 * blocks - 1) - (blocks - 1)
    per_delta = lax.optimization_barrier(jnp.sum(mask[None] * (apart[None] == deltas[:, None, None]).astype(jnp.int32), axis=(1, 2)))
    offsets = columns - C
    intersection = jnp.maximum(0, width - jnp.abs(offsets[:, None] - width * deltas[None, :]))
    return lax.optimization_barrier(jnp.sum(intersection * per_delta[None, :], axis=1))

def stack_scale(counts):
    return 1.0 / jnp.sqrt(NB * jnp.maximum(counts, 1).astype(jnp.float32))

def reference(raw, mask):
    spectrum = jnp.fft.rfft(raw, axis=0)[K0:K0 + NB]
    real_spec = jnp.real(spectrum).astype(jnp.float32).T
    imag_spec = jnp.imag(spectrum).astype(jnp.float32).T
    amplitude = jnp.sqrt(real_spec * real_spec + imag_spec * imag_spec)
    smooth = moving_mean(jnp.pad(amplitude, ((0, 0), (SW, SW))))
    weights = taper_weights(0, NB)
    real_white = (real_spec * weights[None, :] / (smooth + EPS)).astype(jnp.bfloat16)
    imag_white = (imag_spec * weights[None, :] / (smooth + EPS)).astype(jnp.bfloat16)
    phases = lag_phases(K0 + lax.iota(jnp.int32, NB))
    cosines = jnp.cos(phases)
    sines = jnp.sin(phases)
    spectra = jnp.concatenate([real_white, imag_white], axis=1)

    def one_block(total, index):
        row_mask = lax.dynamic_index_in_dim(mask, index, 0, keepdims=False)
        live = jnp.repeat(row_mask, BLOCK_CH).astype(jnp.bfloat16)
        masked = spectra * live[:, None]
        own_real = lax.dynamic_slice_in_dim(real_white, index * BLOCK_CH, BLOCK_CH, 0)[::-1]
        own_imag = lax.dynamic_slice_in_dim(imag_white, index * BLOCK_CH, BLOCK_CH, 0)[::-1]
        rotated = rotate(own_real, own_imag, cosines, sines)
        product = jnp.dot(rotated.astype(jnp.float32), masked.astype(jnp.float32).T, precision=lax.Precision.HIGHEST)
        diagonal = diagonal_sums(product.reshape(LAGS, BLOCK_CH, C), BLOCK_CH)
        first_col = C - BLOCK_CH + 1 - index * BLOCK_CH
        return (place(total, diagonal, first_col), None)
    total, _ = lax.scan(one_block, jnp.zeros((LAGS, OFFSETS), jnp.float32), lax.iota(jnp.int32, BLOCKS))
    counts = pair_counts(mask, lax.iota(jnp.int32, OFFSETS))
    return total * stack_scale(counts)[None, :]
```

```python
import functools
import math

import jax
import jax.numpy as jnp
import ml_dtypes
import numpy as np
from jax import lax
from jax.experimental import pallas as pl
from jax.experimental.pallas import tpu as pltpu
from jax.sharding import PartitionSpec as P

NT = 8192
C = 4096
NB = 2048
K0 = 16
SW = 32
TAPER = 128
LAGS = 8
LAG_STEP = 32
EPS = 1e-06

RADIX = 16
SPAN = NT // RADIX
M_ROWS = NB // RADIX
LANES = 128
PAD = 8
bf16 = ml_dtypes.bfloat16


def split_high_low(table):
    high = table.astype(bf16)
    low = (table - high.astype(np.float64)).astype(bf16)
    return high, low


@functools.cache
def spectrum_tables():
    m = np.arange(M_ROWS)[:, None] + 1
    s = np.arange(SPAN)[None, :]

    def waves(rho):
        angle = 2 * np.pi * (((RADIX * m + rho) * s) % NT) / NT
        return np.cos(angle), np.sin(angle)

    zero = np.zeros((M_ROWS, SPAN))
    tables = []
    c0, s0 = waves(0)
    c8, s8 = waves(RADIX // 2)
    tables.append(np.block([[c0, zero], [-s0, zero], [zero, c8], [zero, -s8]]))
    for rho in range(1, RADIX // 2):
        ca, sa = waves(rho)
        cb, sb = waves(RADIX - rho)
        tables.append(np.block([[ca, sa], [-sa, ca], [cb, -sb], [-sb, -cb]]))
    return np.stack(tables).astype(bf16)


@functools.cache
def taper_table():
    j = np.arange(NB, dtype=np.float64)
    edge = np.minimum(j, NB - 1 - j)
    weights = np.where(edge < TAPER, 0.5 - 0.5 * np.cos(math.pi * (edge + 0.5) / TAPER), 1.0)
    weights = weights.reshape(M_ROWS, RADIX).T
    return np.ascontiguousarray(weights.astype(np.float32)[:, :, None])


@functools.cache
def channel_tables(width, chunk):
    size = 2 * width
    c = np.arange(width)[:, None]
    q = np.arange(size)[None, :]
    angle = 2 * np.pi * ((c * q) % size) / size
    both = np.stack([np.cos(angle), np.sin(angle)], axis=1).reshape(width, 2, size // chunk, chunk)
    both = both.transpose(2, 0, 1, 3).reshape(size // chunk, width, 2 * chunk)
    return split_high_low(both)


@functools.cache
def offset_tables(width, chunk):
    size = 2 * width
    q = np.arange(size)[:, None]
    d = np.arange(size)[None, :] - width
    angle = 2 * np.pi * ((q * d) % size) / size
    both = np.stack([np.cos(angle), np.sin(angle)]) / size
    both[:, :, 0] = 0.0
    both = both.reshape(2, size // chunk, chunk, size).transpose(1, 0, 2, 3)
    return split_high_low(both.reshape(size // chunk, 2 * chunk, size))


def real_dft16(x):
    a = [x[h] + x[h + 8] for h in range(8)]
    b = [x[h] - x[h + 8] for h in range(8)]
    out = {}
    lo = [a[h] + a[h + 4] for h in range(4)]
    d = [a[h] - a[h + 4] for h in range(4)]
    out[0] = (lo[0] + lo[2]) + (lo[1] + lo[3])
    out[8] = (lo[0] + lo[2]) - (lo[1] + lo[3])
    out[4] = (lo[0] - lo[2], lo[3] - lo[1])
    root = math.sqrt(0.5)
    minus, plus = (d[1] - d[3]) * root, (d[1] + d[3]) * root
    out[2] = (d[0] + minus, -(d[2] + plus))
    out[6] = (d[0] - minus, d[2] - plus)
    diff = [None] + [b[h] - b[8 - h] for h in range(1, 4)]
    add = [None] + [b[h] + b[8 - h] for h in range(1, 4)]
    for rho in (1, 3, 5, 7):
        re, im = b[0], b[4] * (-math.sin(math.pi * rho / 2))
        for h in range(1, 4):
            re = re + diff[h] * math.cos(math.pi * h * rho / 8)
            im = im - add[h] * math.sin(math.pi * h * rho / 8)
        out[rho] = (re, im)
    return out


def whiten_kernel(groups, series_ref, table_ref, taper_ref, white_ref, y_ref, spec_ref, pre_ref, suf_ref, all_ref):
    step = pl.program_id(0)
    half = RADIX // 2
    rows = 16

    @pl.when(step == 0)
    def _():
        @pl.loop(0, SPAN // rows)
        def _(i):
            start = pl.multiple_of(i * rows, rows)
            x = [
                series_ref[pl.ds(pl.multiple_of(h * SPAN + start, rows), rows), :].astype(jnp.float32)
                for h in range(RADIX)
            ]
            y = real_dft16(x)
            y[0] = (y[0], y[half])
            for rho in range(half):
                for part in range(2):
                    y_ref[rho, pl.ds(pl.multiple_of(part * SPAN + start, rows), rows), :] = y[rho][part].astype(
                        jnp.bfloat16
                    )

    both = jnp.dot(table_ref[0], y_ref[step], preferred_element_type=jnp.float32)
    other = jnp.where(step == 0, half, RADIX - step)
    spec_ref[step] = both[: 2 * M_ROWS]
    spec_ref[other] = both[2 * M_ROWS :]

    @pl.when(step == half - 1)
    def _():
        chans = series_ref.shape[1]
        edge = jnp.zeros((PAD, chans), jnp.float32)
        inner = pl.ds(PAD, M_ROWS)

        def amplitude(rho):
            re = spec_ref[rho, pl.ds(0, M_ROWS), :]
            im = spec_ref[rho, pl.ds(M_ROWS, M_ROWS), :]
            return jnp.sqrt(re * re + im * im)

        for ref, order in ((pre_ref, range(RADIX)), (suf_ref, range(RADIX - 1, -1, -1))):
            for n, rho in enumerate(order):
                ref[rho, pl.ds(0, PAD), :] = edge
                ref[rho, pl.ds(PAD + M_ROWS, PAD), :] = edge
                if ref is pre_ref:
                    amp = amplitude(rho)
                    spec_amp = amp if n == 0 else ref[rho - 1, inner, :] + amp
                    ref[rho, inner, :] = spec_amp
                    suf_ref[rho, inner, :] = amp
                elif n > 0:
                    ref[rho, inner, :] = ref[rho, inner, :] + ref[rho + 1, inner, :]
        last = RADIX - 1
        all_ref[...] = (
            pre_ref[last, pl.ds(PAD - 1, M_ROWS), :]
            + pre_ref[last, inner, :]
            + pre_ref[last, pl.ds(PAD + 1, M_ROWS), :]
        )
        per = M_ROWS // groups
        for rho in range(RADIX):
            total = all_ref[...] + suf_ref[rho, pl.ds(PAD - 2, M_ROWS), :] + pre_ref[rho, pl.ds(PAD + 2, M_ROWS), :]
            scale = taper_ref[rho] / (total / (2 * SW + 1) + EPS)
            for part in range(2):
                value = (spec_ref[rho, pl.ds(part * M_ROWS, M_ROWS), :] * scale).astype(jnp.bfloat16)
                for g in range(groups):
                    white_ref[rho * groups + g, part] = value[g * per : (g + 1) * per]


def whiten(series, n_dev):
    chans = series.shape[1]
    groups = n_dev // RADIX
    half = RADIX // 2
    out = jax.ShapeDtypeStruct((n_dev, 2, M_ROWS // groups, chans), jnp.bfloat16)
    return pl.pallas_call(
        functools.partial(whiten_kernel, groups),
        grid=(half,),
        out_shape=out,
        in_specs=[
            pl.BlockSpec(series.shape, lambda i: (0, 0)),
            pl.BlockSpec((1, 4 * M_ROWS, 2 * SPAN), lambda i: (i, 0, 0)),
            pl.BlockSpec((RADIX, M_ROWS, 1), lambda i: (0, 0, 0)),
        ],
        out_specs=pl.BlockSpec(out.shape, lambda i: (0, 0, 0, 0)),
        scratch_shapes=[
            pltpu.VMEM((half, 2 * SPAN, chans), jnp.bfloat16),
            pltpu.VMEM((RADIX, 2 * M_ROWS, chans), jnp.float32),
            pltpu.VMEM((RADIX, M_ROWS + 2 * PAD, chans), jnp.float32),
            pltpu.VMEM((RADIX, M_ROWS + 2 * PAD, chans), jnp.float32),
            pltpu.VMEM((M_ROWS, chans), jnp.float32),
        ],
        compiler_params=pltpu.CompilerParams(vmem_limit_bytes=40 * 2**20),
        cost_estimate=pl.CostEstimate(flops=2 * 8 * 512 * 1024 * chans, bytes_accessed=12 * 2**20, transcendentals=0),
        name="whiten",
    )(series, jnp.asarray(spectrum_tables()), jnp.asarray(taper_table()))


def split_rounded(value):
    high = value.astype(jnp.bfloat16)
    return high, (value - high.astype(jnp.float32)).astype(jnp.bfloat16)


def correlate_kernel(
    blocks, mask_ref, white_ref, waves_ref, high_ref, low_ref, back_high_ref, back_low_ref, out_ref, lhs_ref, re_ref, im_ref, h_ref, acc_ref
):
    step = pl.program_id(0)
    sources, _, bins, chans = white_ref.shape
    per_block = sources // blocks
    chunk = re_ref.shape[2]
    width = per_block * chans
    f32 = jnp.float32

    @pl.when(step == 0)
    def _():
        acc_ref[...] = jnp.zeros_like(acc_ref)
        for s in range(sources):
            block, place = divmod(s, per_block)
            for part in range(2):
                lhs_ref[pl.ds((2 * block + part) * bins, bins), pl.ds(place * chans, chans)] = white_ref[s, part]

    for block in range(blocks):
        lhs = lhs_ref[pl.ds(2 * block * bins, 2 * bins), :]
        product = jnp.dot(lhs, high_ref[0], preferred_element_type=f32)
        product = product + jnp.dot(lhs, low_ref[0], preferred_element_type=f32)
        re_ref[block] = product[:bins, :chunk] + product[bins:, chunk:]
        im_ref[block] = product[bins:, :chunk] - product[:bins, chunk:]

    half = LAGS // 2
    zero_row = (blocks - 1) * LAGS
    for delta in range(blocks):
        sums = [jnp.zeros((8, chunk), f32) for _ in range(4 * half)]
        for b in range(bins // 8):
            rows = pl.ds(8 * b, 8)
            g_re = jnp.zeros((8, chunk), f32)
            g_im = jnp.zeros((8, chunk), f32)
            for block in range(blocks - delta):
                keep = mask_ref[block, block + delta]
                a_re, a_im = re_ref[block, rows, :], im_ref[block, rows, :]
                if delta == 0:
                    g_re = g_re + keep * (a_re * a_re + a_im * a_im)
                else:
                    b_re, b_im = re_ref[block + delta, rows, :], im_ref[block + delta, rows, :]
                    g_re = g_re + keep * (a_re * b_re + a_im * b_im)
                    g_im = g_im + keep * (a_im * b_re - a_re * b_im)
            for j in range(half):
                cosine, sine = waves_ref[j, rows, :], waves_ref[half + j, rows, :]
                sums[4 * j] = sums[4 * j] + cosine * g_re
                sums[4 * j + 1] = sums[4 * j + 1] + sine * g_re
                if delta > 0:
                    sums[4 * j + 2] = sums[4 * j + 2] + cosine * g_im
                    sums[4 * j + 3] = sums[4 * j + 3] + sine * g_im
        sums = [jnp.sum(value, axis=0, keepdims=True) for value in sums]
        h_re, h_im = [None] * LAGS, [None] * LAGS
        for j in range(half):
            cr, sr, ci, si = sums[4 * j : 4 * j + 4]
            h_re[half + j], h_im[half + j] = cr - si, ci + sr
            h_re[half - 1 - j], h_im[half - 1 - j] = cr + si, ci - sr
        ahead = zero_row + delta * LAGS
        h_ref[pl.ds(ahead, LAGS), pl.ds(0, chunk)] = jnp.concatenate(h_re, axis=0)
        h_ref[pl.ds(ahead, LAGS), pl.ds(chunk, chunk)] = jnp.concatenate(h_im, axis=0)
        if delta > 0:
            behind = zero_row - delta * LAGS
            h_ref[pl.ds(behind, LAGS), pl.ds(0, chunk)] = jnp.concatenate(h_re[::-1], axis=0)
            h_ref[pl.ds(behind, LAGS), pl.ds(chunk, chunk)] = -jnp.concatenate(h_im[::-1], axis=0)

    h_high, h_low = split_rounded(h_ref[...])
    acc_ref[...] += (
        jnp.dot(h_high, back_high_ref[0], preferred_element_type=f32)
        + jnp.dot(h_low, back_high_ref[0], preferred_element_type=f32)
        + jnp.dot(h_high, back_low_ref[0], preferred_element_type=f32)
    )

    @pl.when(step == pl.num_programs(0) - 1)
    def _():
        devices, _, cols = out_ref.shape
        parts = width // cols
        for segment in range(2 * blocks):
            value = jnp.zeros((LAGS, width), f32)
            if segment < 2 * blocks - 1:
                value = value + acc_ref[pl.ds(segment * LAGS, LAGS), pl.ds(0, width)]
            if segment > 0:
                value = value + acc_ref[pl.ds((segment - 1) * LAGS, LAGS), pl.ds(width, width)]
            for part in range(parts):
                out_ref[segment * parts + part] = value[:, part * cols : (part + 1) * cols]


def correlate(white, mask, waves):
    n_dev, _, bins, chans = white.shape
    blocks = mask.shape[0]
    width = C // blocks
    size = 2 * width
    chunk = LANES
    high, low = channel_tables(width, chunk)
    back_high, back_low = offset_tables(width, chunk)
    rows = (2 * blocks - 1) * LAGS
    out = jax.ShapeDtypeStruct((n_dev, LAGS, 2 * C // n_dev), jnp.float32)
    table = pl.BlockSpec((1, width, 2 * chunk), lambda i: (i, 0, 0))
    back = pl.BlockSpec((1, 2 * chunk, size), lambda i: (i, 0, 0))
    return pl.pallas_call(
        functools.partial(correlate_kernel, blocks),
        grid=(size // chunk,),
        out_shape=out,
        in_specs=[
            pl.BlockSpec(memory_space=pltpu.SMEM),
            pl.BlockSpec(white.shape, lambda i: (0, 0, 0, 0)),
            pl.BlockSpec(waves.shape, lambda i: (0, 0, 0)),
            table,
            table,
            back,
            back,
        ],
        out_specs=pl.BlockSpec(out.shape, lambda i: (0, 0, 0)),
        scratch_shapes=[
            pltpu.VMEM((blocks * 2 * bins, width), jnp.bfloat16),
            pltpu.VMEM((blocks, bins, chunk), jnp.float32),
            pltpu.VMEM((blocks, bins, chunk), jnp.float32),
            pltpu.VMEM((rows, 2 * chunk), jnp.float32),
            pltpu.VMEM((rows, size), jnp.float32),
        ],
        compiler_params=pltpu.CompilerParams(vmem_limit_bytes=40 * 2**20),
        cost_estimate=pl.CostEstimate(flops=5 * 2**30, bytes_accessed=14 * 2**20, transcendentals=0),
        name="correlate",
    )(
        mask.astype(jnp.float32),
        white,
        waves,
        jnp.asarray(high),
        jnp.asarray(low),
        jnp.asarray(back_high),
        jnp.asarray(back_low),
    )


def lag_waves(device, bins, groups):
    rho, group = device // groups, device % groups
    k = RADIX * (group * bins + lax.iota(jnp.int32, bins) + 1) + rho
    number = lax.iota(jnp.int32, LAGS // 2) + LAGS // 2
    shifts = LAG_STEP * (2 * number + 1 - LAGS) // 2
    phase = jnp.mod(shifts[:, None] * k[None, :], NT).astype(jnp.float32) * (2 * math.pi / NT)
    waves = jnp.concatenate([jnp.cos(phase), jnp.sin(phase)], axis=0)
    return jnp.broadcast_to(waves[:, :, None], (LAGS, bins, LANES))


def pair_counts(mask, columns):
    blocks = mask.shape[0]
    width = C // blocks
    labels = lax.iota(jnp.int32, blocks)
    apart = labels[None, :] - labels[:, None]
    deltas = lax.iota(jnp.int32, 2 * blocks - 1) - (blocks - 1)
    per_delta = jnp.sum(
        mask[None] * (apart[None] == deltas[:, None, None]).astype(jnp.int32), axis=(1, 2)
    )
    offsets = columns - C
    intersection = jnp.maximum(0, width - jnp.abs(offsets[:, None] - width * deltas[None, :]))
    return jnp.sum(intersection * per_delta[None, :], axis=1)


def stack_scale(counts):
    return 1.0 / jnp.sqrt(NB * jnp.maximum(counts, 1).astype(jnp.float32))


def on_device(raw, mask):
    axes = ("blk", "lag")
    n_dev = lax.axis_size("blk") * lax.axis_size("lag")
    device = lax.axis_index("blk") * lax.axis_size("lag") + lax.axis_index("lag")
    series = lax.all_to_all(raw.astype(jnp.bfloat16), axes, split_axis=1, concat_axis=0, tiled=True)
    white = whiten(series, n_dev)
    waves = lag_waves(device, white.shape[2], n_dev // RADIX)
    white = lax.all_to_all(white, axes, split_axis=0, concat_axis=0, tiled=True)
    partial = correlate(white, mask, waves)
    shares = lax.all_to_all(partial, axes, split_axis=0, concat_axis=0, tiled=True)
    total = jnp.sum(shares, axis=0)
    n_cols = total.shape[1]
    counts = pair_counts(mask, device * n_cols + lax.iota(jnp.int32, n_cols))
    return total * stack_scale(counts)[None, :]


def solution(mesh):
    return jax.shard_map(
        on_device,
        mesh=mesh,
        in_specs=(P(("blk", "lag"), None), P()),
        out_specs=P(None, ("blk", "lag")),
        check_vma=False,
    )
```

```python
import functools
import math

import jax
import jax.numpy as jnp
import ml_dtypes
import numpy as np
from jax import lax
from jax.experimental import pallas as pl
from jax.experimental.pallas import tpu as pltpu
from jax.sharding import PartitionSpec as P

NT = 8192
C = 4096
NB = 2048
K0 = 16
SW = 32
TAPER = 128
LAGS = 8
LAG_STEP = 32
EPS = 1e-06

RADIX = 16
SPAN = NT // RADIX
M_ROWS = NB // RADIX
LANES = 128
PAD = 8
bf16 = ml_dtypes.bfloat16


def split_high_low(table):
    high = table.astype(bf16)
    low = (table - high.astype(np.float64)).astype(bf16)
    return high, low


@functools.cache
def spectrum_tables():
    m = np.arange(M_ROWS)[:, None] + 1
    s = np.arange(SPAN)[None, :]

    def waves(rho):
        angle = 2 * np.pi * (((RADIX * m + rho) * s) % NT) / NT
        return np.cos(angle), np.sin(angle)

    zero = np.zeros((M_ROWS, SPAN))
    tables = []
    c0, s0 = waves(0)
    c8, s8 = waves(RADIX // 2)
    tables.append(np.block([[c0, zero], [-s0, zero], [zero, c8], [zero, -s8]]))
    for rho in range(1, RADIX // 2):
        ca, sa = waves(rho)
        cb, sb = waves(RADIX - rho)
        tables.append(np.block([[ca, sa], [-sa, ca], [cb, -sb], [-sb, -cb]]))
    return np.stack(tables).astype(bf16)


@functools.cache
def taper_table():
    j = np.arange(NB, dtype=np.float64)
    edge = np.minimum(j, NB - 1 - j)
    weights = np.where(edge < TAPER, 0.5 - 0.5 * np.cos(math.pi * (edge + 0.5) / TAPER), 1.0)
    weights = weights.reshape(M_ROWS, RADIX).T
    return np.ascontiguousarray(weights.astype(np.float32)[:, :, None])


@functools.cache
def channel_tables(width, chunk):
    size = 2 * width
    c = np.arange(width)[:, None]
    q = np.arange(size)[None, :]
    angle = 2 * np.pi * ((c * q) % size) / size
    both = np.stack([np.cos(angle), np.sin(angle)], axis=1).reshape(width, 2, size // chunk, chunk)
    both = both.transpose(2, 0, 1, 3).reshape(size // chunk, width, 2 * chunk)
    return split_high_low(both)


@functools.cache
def offset_tables(width, chunk):
    size = 2 * width
    q = np.arange(size)[:, None]
    d = np.arange(size)[None, :] - width
    angle = 2 * np.pi * ((q * d) % size) / size
    both = np.stack([np.cos(angle), np.sin(angle)]) / size
    both[:, :, 0] = 0.0
    both = both.reshape(2, size // chunk, chunk, size).transpose(1, 0, 2, 3)
    return split_high_low(both.reshape(size // chunk, 2 * chunk, size))


def real_dft16(x):
    a = [x[h] + x[h + 8] for h in range(8)]
    b = [x[h] - x[h + 8] for h in range(8)]
    out = {}
    lo = [a[h] + a[h + 4] for h in range(4)]
    d = [a[h] - a[h + 4] for h in range(4)]
    out[0] = (lo[0] + lo[2]) + (lo[1] + lo[3])
    out[8] = (lo[0] + lo[2]) - (lo[1] + lo[3])
    out[4] = (lo[0] - lo[2], lo[3] - lo[1])
    root = math.sqrt(0.5)
    minus, plus = (d[1] - d[3]) * root, (d[1] + d[3]) * root
    out[2] = (d[0] + minus, -(d[2] + plus))
    out[6] = (d[0] - minus, d[2] - plus)
    diff = [None] + [b[h] - b[8 - h] for h in range(1, 4)]
    add = [None] + [b[h] + b[8 - h] for h in range(1, 4)]
    for rho in (1, 3, 5, 7):
        re, im = b[0], b[4] * (-math.sin(math.pi * rho / 2))
        for h in range(1, 4):
            re = re + diff[h] * math.cos(math.pi * h * rho / 8)
            im = im - add[h] * math.sin(math.pi * h * rho / 8)
        out[rho] = (re, im)
    return out


def own_index():
    return lax.axis_index("blk") * lax.axis_size("lag") + lax.axis_index("lag")


def coordinates(device):
    n_lag = lax.axis_size("lag")
    return (device // n_lag, device % n_lag)


def greet_all(n_dev):
    barrier = pltpu.get_barrier_semaphore()
    me = own_index()

    @pl.loop(1, n_dev)
    def _(ahead):
        other = (me + ahead) % n_dev
        pl.semaphore_signal(barrier, inc=1, device_id=coordinates(other), device_id_type=pl.DeviceIdType.MESH)


def meet_all(n_dev):
    pl.semaphore_wait(pltpu.get_barrier_semaphore(), n_dev - 1)


def slot_copy(src_ref, dst_ref, src, dst, send_sem, recv_sem, device):
    return pltpu.make_async_remote_copy(
        src_ref=src_ref.at[src],
        dst_ref=dst_ref.at[dst],
        send_sem=send_sem.at[src],
        recv_sem=recv_sem.at[dst],
        device_id=coordinates(device),
        device_id_type=pl.DeviceIdType.MESH,
    )


def start_all(n_dev, src_ref, dst_ref, send_sem, recv_sem):
    me = own_index()

    @pl.loop(1, n_dev)
    def _(ahead):
        other = (me + ahead) % n_dev
        slot_copy(src_ref, dst_ref, other, me, send_sem, recv_sem, other).start()


def wait_all(n_dev, src_ref, dst_ref, send_sem, recv_sem):
    me = own_index()

    @pl.loop(1, n_dev)
    def _(ahead):
        other = (me + ahead) % n_dev
        copy = slot_copy(src_ref, dst_ref, other, other, send_sem, recv_sem, other)
        copy.wait_send()
        copy.wait_recv()


def whiten_kernel(
    groups,
    raw_ref,
    table_ref,
    taper_ref,
    white_ref,
    cast_ref,
    series_ref,
    ready_ref,
    y_ref,
    spec_ref,
    pre_ref,
    suf_ref,
    all_ref,
    raw_send,
    raw_recv,
    white_send,
    white_recv,
    own_sem,
):
    step = pl.program_id(0)
    half = RADIX // 2
    rows = 16
    n_dev, samples, chans = series_ref.shape
    me = own_index()

    @pl.when(step == 0)
    def _():
        greet_all(n_dev)
        for other in range(n_dev):
            cast_ref[other] = raw_ref[:, other * chans : (other + 1) * chans].astype(jnp.bfloat16)
        meet_all(n_dev)
        start_all(n_dev, cast_ref, series_ref, raw_send, raw_recv)
        series_ref[me] = cast_ref[me]
        wait_all(n_dev, cast_ref, series_ref, raw_send, raw_recv)
        pieces = SPAN // samples
        per_piece = samples // rows

        @pl.loop(0, SPAN // rows)
        def _(i):
            start = pl.multiple_of(i * rows, rows)
            piece = i // per_piece
            inside = pl.multiple_of((i % per_piece) * rows, rows)
            x = [
                series_ref[h * pieces + piece, pl.ds(inside, rows), :].astype(jnp.float32) for h in range(RADIX)
            ]
            y = real_dft16(x)
            y[0] = (y[0], y[half])
            for rho in range(half):
                for part in range(2):
                    y_ref[rho, pl.ds(pl.multiple_of(part * SPAN + start, rows), rows), :] = y[rho][part].astype(
                        jnp.bfloat16
                    )

    both = jnp.dot(table_ref[0], y_ref[step], preferred_element_type=jnp.float32)
    other = jnp.where(step == 0, half, RADIX - step)
    spec_ref[step] = both[: 2 * M_ROWS]
    spec_ref[other] = both[2 * M_ROWS :]

    @pl.when(step == half - 1)
    def _():
        edge = jnp.zeros((PAD, chans), jnp.float32)
        inner = pl.ds(PAD, M_ROWS)

        def amplitude(rho):
            re = spec_ref[rho, pl.ds(0, M_ROWS), :]
            im = spec_ref[rho, pl.ds(M_ROWS, M_ROWS), :]
            return jnp.sqrt(re * re + im * im)

        for ref, order in ((pre_ref, range(RADIX)), (suf_ref, range(RADIX - 1, -1, -1))):
            for n, rho in enumerate(order):
                ref[rho, pl.ds(0, PAD), :] = edge
                ref[rho, pl.ds(PAD + M_ROWS, PAD), :] = edge
                if ref is pre_ref:
                    amp = amplitude(rho)
                    spec_amp = amp if n == 0 else ref[rho - 1, inner, :] + amp
                    ref[rho, inner, :] = spec_amp
                    suf_ref[rho, inner, :] = amp
                elif n > 0:
                    ref[rho, inner, :] = ref[rho, inner, :] + ref[rho + 1, inner, :]
        last = RADIX - 1
        all_ref[...] = (
            pre_ref[last, pl.ds(PAD - 1, M_ROWS), :]
            + pre_ref[last, inner, :]
            + pre_ref[last, pl.ds(PAD + 1, M_ROWS), :]
        )
        per = M_ROWS // groups

        @pl.loop(0, RADIX)
        def _(i):
            rho = (me // groups + 1 + i) % RADIX
            total = all_ref[...] + suf_ref[rho, pl.ds(PAD - 2, M_ROWS), :] + pre_ref[rho, pl.ds(PAD + 2, M_ROWS), :]
            scale = taper_ref[rho] / (total / (2 * SW + 1) + EPS)
            for part in range(2):
                value = (spec_ref[rho, pl.ds(part * M_ROWS, M_ROWS), :] * scale).astype(jnp.bfloat16)
                for g in range(groups):
                    ready_ref[rho * groups + g, part] = value[g * per : (g + 1) * per]
            for g in range(groups):
                other = rho * groups + g

                @pl.when(other != me)
                def _():
                    slot_copy(ready_ref, white_ref, other, me, white_send, white_recv, other).start()

        own = pltpu.make_async_copy(ready_ref.at[me], white_ref.at[me], own_sem)
        own.start()
        own.wait()
        wait_all(n_dev, ready_ref, white_ref, white_send, white_recv)


def whiten(raw, n_dev):
    samples = raw.shape[0]
    chans = C // n_dev
    groups = n_dev // RADIX
    half = RADIX // 2
    out = jax.ShapeDtypeStruct((n_dev, 2, M_ROWS // groups, chans), jnp.bfloat16)
    return pl.pallas_call(
        functools.partial(whiten_kernel, groups),
        grid=(half,),
        out_shape=out,
        in_specs=[
            pl.BlockSpec(raw.shape, lambda i: (0, 0)),
            pl.BlockSpec((1, 4 * M_ROWS, 2 * SPAN), lambda i: (i, 0, 0)),
            pl.BlockSpec((RADIX, M_ROWS, 1), lambda i: (0, 0, 0)),
        ],
        out_specs=pl.BlockSpec(memory_space=pl.ANY),
        scratch_shapes=[
            pltpu.VMEM((n_dev, samples, chans), jnp.bfloat16),
            pltpu.VMEM((n_dev, samples, chans), jnp.bfloat16),
            pltpu.VMEM(out.shape, jnp.bfloat16),
            pltpu.VMEM((half, 2 * SPAN, chans), jnp.bfloat16),
            pltpu.VMEM((RADIX, 2 * M_ROWS, chans), jnp.float32),
            pltpu.VMEM((RADIX, M_ROWS + 2 * PAD, chans), jnp.float32),
            pltpu.VMEM((RADIX, M_ROWS + 2 * PAD, chans), jnp.float32),
            pltpu.VMEM((M_ROWS, chans), jnp.float32),
            pltpu.SemaphoreType.DMA((n_dev,)),
            pltpu.SemaphoreType.DMA((n_dev,)),
            pltpu.SemaphoreType.DMA((n_dev,)),
            pltpu.SemaphoreType.DMA((n_dev,)),
            pltpu.SemaphoreType.DMA(()),
        ],
        compiler_params=pltpu.CompilerParams(
            vmem_limit_bytes=56 * 2**20, collective_id=0, has_side_effects=True
        ),
        cost_estimate=pl.CostEstimate(flops=2 * 8 * 512 * 1024 * chans, bytes_accessed=12 * 2**20, transcendentals=0),
        name="whiten",
    )(raw, jnp.asarray(spectrum_tables()), jnp.asarray(taper_table()))


def split_rounded(value):
    high = value.astype(jnp.bfloat16)
    return high, (value - high.astype(jnp.float32)).astype(jnp.bfloat16)


def correlate_kernel(
    blocks,
    mask_ref,
    white_ref,
    waves_ref,
    high_ref,
    low_ref,
    back_high_ref,
    back_low_ref,
    out_ref,
    lhs_ref,
    re_ref,
    im_ref,
    h_ref,
    acc_ref,
    part_ref,
    got_ref,
    send_sem,
    recv_sem,
):
    step = pl.program_id(0)
    sources, _, bins, chans = white_ref.shape
    per_block = sources // blocks
    chunk = re_ref.shape[2]
    width = per_block * chans
    f32 = jnp.float32

    @pl.when(step == 0)
    def _():
        greet_all(sources)
        acc_ref[...] = jnp.zeros_like(acc_ref)
        for s in range(sources):
            block, place = divmod(s, per_block)
            for part in range(2):
                lhs_ref[pl.ds((2 * block + part) * bins, bins), pl.ds(place * chans, chans)] = white_ref[s, part]

    for block in range(blocks):
        lhs = lhs_ref[pl.ds(2 * block * bins, 2 * bins), :]
        product = jnp.dot(lhs, high_ref[0], preferred_element_type=f32)
        product = product + jnp.dot(lhs, low_ref[0], preferred_element_type=f32)
        re_ref[block] = product[:bins, :chunk] + product[bins:, chunk:]
        im_ref[block] = product[bins:, :chunk] - product[:bins, chunk:]

    half = LAGS // 2
    zero_row = (blocks - 1) * LAGS
    for delta in range(blocks):
        sums = [jnp.zeros((8, chunk), f32) for _ in range(4 * half)]
        for b in range(bins // 8):
            rows = pl.ds(8 * b, 8)
            g_re = jnp.zeros((8, chunk), f32)
            g_im = jnp.zeros((8, chunk), f32)
            for block in range(blocks - delta):
                keep = mask_ref[block, block + delta]
                a_re, a_im = re_ref[block, rows, :], im_ref[block, rows, :]
                if delta == 0:
                    g_re = g_re + keep * (a_re * a_re + a_im * a_im)
                else:
                    b_re, b_im = re_ref[block + delta, rows, :], im_ref[block + delta, rows, :]
                    g_re = g_re + keep * (a_re * b_re + a_im * b_im)
                    g_im = g_im + keep * (a_im * b_re - a_re * b_im)
            for j in range(half):
                cosine, sine = waves_ref[j, rows, :], waves_ref[half + j, rows, :]
                sums[4 * j] = sums[4 * j] + cosine * g_re
                sums[4 * j + 1] = sums[4 * j + 1] + sine * g_re
                if delta > 0:
                    sums[4 * j + 2] = sums[4 * j + 2] + cosine * g_im
                    sums[4 * j + 3] = sums[4 * j + 3] + sine * g_im
        sums = [jnp.sum(value, axis=0, keepdims=True) for value in sums]
        h_re, h_im = [None] * LAGS, [None] * LAGS
        for j in range(half):
            cr, sr, ci, si = sums[4 * j : 4 * j + 4]
            h_re[half + j], h_im[half + j] = cr - si, ci + sr
            h_re[half - 1 - j], h_im[half - 1 - j] = cr + si, ci - sr
        ahead = zero_row + delta * LAGS
        h_ref[pl.ds(ahead, LAGS), pl.ds(0, chunk)] = jnp.concatenate(h_re, axis=0)
        h_ref[pl.ds(ahead, LAGS), pl.ds(chunk, chunk)] = jnp.concatenate(h_im, axis=0)
        if delta > 0:
            behind = zero_row - delta * LAGS
            h_ref[pl.ds(behind, LAGS), pl.ds(0, chunk)] = jnp.concatenate(h_re[::-1], axis=0)
            h_ref[pl.ds(behind, LAGS), pl.ds(chunk, chunk)] = -jnp.concatenate(h_im[::-1], axis=0)

    h_high, h_low = split_rounded(h_ref[...])
    acc_ref[...] += (
        jnp.dot(h_high, back_high_ref[0], preferred_element_type=f32)
        + jnp.dot(h_low, back_high_ref[0], preferred_element_type=f32)
        + jnp.dot(h_high, back_low_ref[0], preferred_element_type=f32)
    )

    @pl.when(step == pl.num_programs(0) - 1)
    def _():
        devices, _, cols = part_ref.shape
        me = own_index()
        parts = width // cols
        for segment in range(2 * blocks):
            value = jnp.zeros((LAGS, width), f32)
            if segment < 2 * blocks - 1:
                value = value + acc_ref[pl.ds(segment * LAGS, LAGS), pl.ds(0, width)]
            if segment > 0:
                value = value + acc_ref[pl.ds((segment - 1) * LAGS, LAGS), pl.ds(width, width)]
            for part in range(parts):
                part_ref[segment * parts + part] = value[:, part * cols : (part + 1) * cols]
        meet_all(devices)
        start_all(devices, part_ref, got_ref, send_sem, recv_sem)
        got_ref[me] = part_ref[me]
        wait_all(devices, part_ref, got_ref, send_sem, recv_sem)
        out_ref[...] = jnp.sum(got_ref[...], axis=0)


def correlate(white, mask, waves):
    n_dev, _, bins, chans = white.shape
    blocks = mask.shape[0]
    width = C // blocks
    size = 2 * width
    chunk = LANES
    high, low = channel_tables(width, chunk)
    back_high, back_low = offset_tables(width, chunk)
    rows = (2 * blocks - 1) * LAGS
    cols = 2 * C // n_dev
    out = jax.ShapeDtypeStruct((LAGS, cols), jnp.float32)
    table = pl.BlockSpec((1, width, 2 * chunk), lambda i: (i, 0, 0))
    back = pl.BlockSpec((1, 2 * chunk, size), lambda i: (i, 0, 0))
    return pl.pallas_call(
        functools.partial(correlate_kernel, blocks),
        grid=(size // chunk,),
        out_shape=out,
        in_specs=[
            pl.BlockSpec(memory_space=pltpu.SMEM),
            pl.BlockSpec(white.shape, lambda i: (0, 0, 0, 0)),
            pl.BlockSpec(waves.shape, lambda i: (0, 0, 0)),
            table,
            table,
            back,
            back,
        ],
        out_specs=pl.BlockSpec(out.shape, lambda i: (0, 0)),
        scratch_shapes=[
            pltpu.VMEM((blocks * 2 * bins, width), jnp.bfloat16),
            pltpu.VMEM((blocks, bins, chunk), jnp.float32),
            pltpu.VMEM((blocks, bins, chunk), jnp.float32),
            pltpu.VMEM((rows, 2 * chunk), jnp.float32),
            pltpu.VMEM((rows, size), jnp.float32),
            pltpu.VMEM((n_dev, LAGS, cols), jnp.float32),
            pltpu.VMEM((n_dev, LAGS, cols), jnp.float32),
            pltpu.SemaphoreType.DMA((n_dev,)),
            pltpu.SemaphoreType.DMA((n_dev,)),
        ],
        compiler_params=pltpu.CompilerParams(
            vmem_limit_bytes=56 * 2**20, collective_id=1, has_side_effects=True
        ),
        cost_estimate=pl.CostEstimate(flops=5 * 2**30, bytes_accessed=14 * 2**20, transcendentals=0),
        name="correlate",
    )(
        mask.astype(jnp.float32),
        white,
        waves,
        jnp.asarray(high),
        jnp.asarray(low),
        jnp.asarray(back_high),
        jnp.asarray(back_low),
    )


def lag_waves(device, bins, groups):
    rho, group = device // groups, device % groups
    k = RADIX * (group * bins + lax.iota(jnp.int32, bins) + 1) + rho
    number = lax.iota(jnp.int32, LAGS // 2) + LAGS // 2
    shifts = LAG_STEP * (2 * number + 1 - LAGS) // 2
    phase = jnp.mod(shifts[:, None] * k[None, :], NT).astype(jnp.float32) * (2 * math.pi / NT)
    waves = jnp.concatenate([jnp.cos(phase), jnp.sin(phase)], axis=0)
    return jnp.broadcast_to(waves[:, :, None], (LAGS, bins, LANES))


def pair_counts(mask, columns):
    blocks = mask.shape[0]
    width = C // blocks
    labels = lax.iota(jnp.int32, blocks)
    apart = labels[None, :] - labels[:, None]
    deltas = lax.iota(jnp.int32, 2 * blocks - 1) - (blocks - 1)
    per_delta = jnp.sum(
        mask[None] * (apart[None] == deltas[:, None, None]).astype(jnp.int32), axis=(1, 2)
    )
    offsets = columns - C
    intersection = jnp.maximum(0, width - jnp.abs(offsets[:, None] - width * deltas[None, :]))
    return jnp.sum(intersection * per_delta[None, :], axis=1)


def stack_scale(counts):
    return 1.0 / jnp.sqrt(NB * jnp.maximum(counts, 1).astype(jnp.float32))


def on_device(raw, mask):
    n_dev = lax.axis_size("blk") * lax.axis_size("lag")
    device = own_index()
    white = whiten(raw, n_dev)
    waves = lag_waves(device, white.shape[2], n_dev // RADIX)
    total = correlate(white, mask, waves)
    n_cols = total.shape[1]
    counts = pair_counts(mask, device * n_cols + lax.iota(jnp.int32, n_cols))
    return total * stack_scale(counts)[None, :]


def solution(mesh):
    return jax.shard_map(
        on_device,
        mesh=mesh,
        in_specs=(P(("blk", "lag"), None), P()),
        out_specs=P(None, ("blk", "lag")),
        check_vma=False,
    )
```

```python
import functools
import math

import jax
import jax.numpy as jnp
import ml_dtypes
import numpy as np
from jax import lax
from jax.experimental import pallas as pl
from jax.experimental.pallas import tpu as pltpu
from jax.sharding import PartitionSpec as P

NT = 8192
C = 4096
NB = 2048
K0 = 16
SW = 32
TAPER = 128
LAGS = 8
LAG_STEP = 32
EPS = 1e-06

RADIX = 16
RAW_CHUNKS = 4
BIN_CHUNK = 16
SPAN = NT // RADIX
M_ROWS = NB // RADIX
LANES = 128
PAD = 8
bf16 = ml_dtypes.bfloat16


def split_high_low(table):
    high = table.astype(bf16)
    low = (table - high.astype(np.float64)).astype(bf16)
    return high, low


@functools.cache
def spectrum_tables(samples):
    m = np.arange(M_ROWS)[:, None] + 1
    s = np.arange(SPAN)[None, :]

    def waves(rho):
        angle = 2 * np.pi * (((RADIX * m + rho) * s) % NT) / NT
        return np.cos(angle), np.sin(angle)

    zero = np.zeros((M_ROWS, SPAN))
    tables = []
    c0, s0 = waves(0)
    c8, s8 = waves(RADIX // 2)
    tables.append(np.block([[c0, zero], [-s0, zero], [zero, c8], [zero, -s8]]))
    for rho in range(1, RADIX // 2):
        ca, sa = waves(rho)
        cb, sb = waves(RADIX - rho)
        tables.append(np.block([[ca, sa], [-sa, ca], [cb, -sb], [-sb, -cb]]))
    table = np.stack(tables).astype(bf16)
    rows = samples // RAW_CHUNKS
    shape = (RADIX // 2, 4 * M_ROWS, 2, SPAN // samples, RAW_CHUNKS, rows)
    table = table.reshape(shape).transpose(4, 0, 1, 2, 3, 5)
    return table.reshape(RAW_CHUNKS, RADIX // 2, 4 * M_ROWS, 2 * SPAN // RAW_CHUNKS)


@functools.cache
def taper_table():
    j = np.arange(NB, dtype=np.float64)
    edge = np.minimum(j, NB - 1 - j)
    weights = np.where(edge < TAPER, 0.5 - 0.5 * np.cos(math.pi * (edge + 0.5) / TAPER), 1.0)
    weights = weights.reshape(M_ROWS, RADIX).T
    return np.ascontiguousarray(weights.astype(np.float32)[:, :, None])


@functools.cache
def channel_tables(width, chunk):
    size = 2 * width
    c = np.arange(width)[:, None]
    q = np.arange(size)[None, :]
    angle = 2 * np.pi * ((c * q) % size) / size
    both = np.stack([np.cos(angle), np.sin(angle)], axis=1).reshape(width, 2, size // chunk, chunk)
    both = both.transpose(2, 0, 1, 3).reshape(size // chunk, width, 2 * chunk)
    return split_high_low(both)


@functools.cache
def offset_tables(width, chunk):
    size = 2 * width
    q = np.arange(size)[:, None]
    d = np.arange(size)[None, :] - width
    angle = 2 * np.pi * ((q * d) % size) / size
    both = np.stack([np.cos(angle), np.sin(angle)]) / size
    both[:, :, 0] = 0.0
    both = both.reshape(2, size // chunk, chunk, size).transpose(1, 0, 2, 3)
    return split_high_low(both.reshape(size // chunk, 2 * chunk, size))


def real_dft16(x):
    a = [x[h] + x[h + 8] for h in range(8)]
    b = [x[h] - x[h + 8] for h in range(8)]
    out = {}
    lo = [a[h] + a[h + 4] for h in range(4)]
    d = [a[h] - a[h + 4] for h in range(4)]
    out[0] = (lo[0] + lo[2]) + (lo[1] + lo[3])
    out[8] = (lo[0] + lo[2]) - (lo[1] + lo[3])
    out[4] = (lo[0] - lo[2], lo[3] - lo[1])
    root = math.sqrt(0.5)
    minus, plus = (d[1] - d[3]) * root, (d[1] + d[3]) * root
    out[2] = (d[0] + minus, -(d[2] + plus))
    out[6] = (d[0] - minus, d[2] - plus)
    diff = [None] + [b[h] - b[8 - h] for h in range(1, 4)]
    add = [None] + [b[h] + b[8 - h] for h in range(1, 4)]
    for rho in (1, 3, 5, 7):
        re, im = b[0], b[4] * (-math.sin(math.pi * rho / 2))
        for h in range(1, 4):
            re = re + diff[h] * math.cos(math.pi * h * rho / 8)
            im = im - add[h] * math.sin(math.pi * h * rho / 8)
        out[rho] = (re, im)
    return out


def own_index():
    return lax.axis_index("blk") * lax.axis_size("lag") + lax.axis_index("lag")


def coordinates(device):
    n_lag = lax.axis_size("lag")
    return (device // n_lag, device % n_lag)


def greet_all(n_dev):
    barrier = pltpu.get_barrier_semaphore()
    me = own_index()

    @pl.loop(1, n_dev)
    def _(ahead):
        other = (me + ahead) % n_dev
        pl.semaphore_signal(barrier, inc=1, device_id=coordinates(other), device_id_type=pl.DeviceIdType.MESH)


def meet_all(n_dev):
    pl.semaphore_wait(pltpu.get_barrier_semaphore(), n_dev - 1)


def split_rounded(value):
    high = value.astype(jnp.bfloat16)
    return high, (value - high.astype(jnp.float32)).astype(jnp.bfloat16)


def slot_copy(src_ref, dst_ref, chunk, src, dst, send_sem, recv_sem, device):
    return pltpu.make_async_remote_copy(
        src_ref=src_ref.at[chunk, src],
        dst_ref=dst_ref.at[chunk, dst],
        send_sem=send_sem.at[chunk, src],
        recv_sem=recv_sem.at[chunk, dst],
        device_id=coordinates(device),
        device_id_type=pl.DeviceIdType.MESH,
    )


def start_all(n_dev, chunk, src_ref, dst_ref, send_sem, recv_sem):
    me = own_index()

    @pl.loop(1, n_dev)
    def _(ahead):
        other = (me + ahead) % n_dev
        slot_copy(src_ref, dst_ref, chunk, other, me, send_sem, recv_sem, other).start()


def wait_all(n_dev, chunk, src_ref, dst_ref, send_sem, recv_sem):
    me = own_index()

    @pl.loop(1, n_dev)
    def _(ahead):
        other = (me + ahead) % n_dev
        copy = slot_copy(src_ref, dst_ref, chunk, other, other, send_sem, recv_sem, other)
        copy.wait_send()
        copy.wait_recv()


def transform(series_ref, chunk, y_ref, spec_ref, table_ref):
    half = RADIX // 2
    tile = 16
    _, n_dev, rows, _ = series_ref.shape
    pieces = n_dev // RADIX
    span = pieces * rows
    per_piece = rows // tile

    @pl.loop(0, span // tile)
    def _(i):
        start = pl.multiple_of(i * tile, tile)
        inside = pl.multiple_of((i % per_piece) * tile, tile)
        x = [
            series_ref[chunk, h * pieces + i // per_piece, pl.ds(inside, tile), :].astype(jnp.float32)
            for h in range(RADIX)
        ]
        y = real_dft16(x)
        y[0] = (y[0], y[half])
        for rho in range(half):
            for part in range(2):
                y_ref[rho, pl.ds(part * span + start, tile), :] = y[rho][part].astype(jnp.bfloat16)

    @pl.loop(0, half)
    def _(pair):
        both = jnp.dot(table_ref[chunk, pair], y_ref[pair], preferred_element_type=jnp.float32)
        other = jnp.where(pair == 0, half, RADIX - pair)
        spec_ref[pair] += both[: 2 * M_ROWS]
        spec_ref[other] += both[2 * M_ROWS :]


def window_sums(spec_ref, pre_ref, suf_ref, all_ref):
    edge = jnp.zeros((PAD, all_ref.shape[1]), jnp.float32)
    inner = pl.ds(PAD, M_ROWS)
    for rho in range(RADIX):
        re = spec_ref[rho, pl.ds(0, M_ROWS), :]
        im = spec_ref[rho, pl.ds(M_ROWS, M_ROWS), :]
        amp = jnp.sqrt(re * re + im * im)
        suf_ref[rho, inner, :] = amp
        pre_ref[rho, inner, :] = amp if rho == 0 else pre_ref[rho - 1, inner, :] + amp
        for ref in (pre_ref, suf_ref):
            ref[rho, pl.ds(0, PAD), :] = edge
            ref[rho, pl.ds(PAD + M_ROWS, PAD), :] = edge
    for rho in range(RADIX - 2, -1, -1):
        suf_ref[rho, inner, :] = suf_ref[rho, inner, :] + suf_ref[rho + 1, inner, :]
    last = RADIX - 1
    all_ref[...] = (
        pre_ref[last, pl.ds(PAD - 1, M_ROWS), :]
        + pre_ref[last, inner, :]
        + pre_ref[last, pl.ds(PAD + 1, M_ROWS), :]
    )


def cross_spectra(blocks, bin_chunk, q, mask_ref, waves_ref, lhs_ref, high_ref, low_ref, re_ref, im_ref, sums_ref):
    f32 = jnp.float32
    half = LAGS // 2
    chunk = re_ref.shape[2]
    bins = BIN_CHUNK
    lhs = lhs_ref[...]
    product = jnp.dot(lhs, high_ref[q], preferred_element_type=f32)
    product = product + jnp.dot(lhs, low_ref[q], preferred_element_type=f32)
    for block in range(blocks):
        real = product[2 * block * bins : (2 * block + 1) * bins]
        imag = product[(2 * block + 1) * bins : (2 * block + 2) * bins]
        re_ref[block] = real[:, :chunk] + imag[:, chunk:]
        im_ref[block] = imag[:, :chunk] - real[:, chunk:]
    for delta in range(blocks):
        sums = [sums_ref[q, delta * 4 * half + n] for n in range(4 * half)]
        for b in range(bins // 8):
            rows = pl.ds(8 * b, 8)
            wave_rows = pl.ds(pl.multiple_of(bin_chunk * bins + 8 * b, 8), 8)
            g_re = jnp.zeros((8, chunk), f32)
            g_im = jnp.zeros((8, chunk), f32)
            for block in range(blocks - delta):
                keep = mask_ref[block, block + delta]
                a_re, a_im = re_ref[block, rows, :], im_ref[block, rows, :]
                if delta == 0:
                    g_re = g_re + keep * (a_re * a_re + a_im * a_im)
                else:
                    b_re, b_im = re_ref[block + delta, rows, :], im_ref[block + delta, rows, :]
                    g_re = g_re + keep * (a_re * b_re + a_im * b_im)
                    g_im = g_im + keep * (a_im * b_re - a_re * b_im)
            for j in range(half):
                cosine, sine = waves_ref[j, wave_rows, :], waves_ref[half + j, wave_rows, :]
                sums[4 * j] = sums[4 * j] + cosine * g_re
                sums[4 * j + 1] = sums[4 * j + 1] + sine * g_re
                if delta > 0:
                    sums[4 * j + 2] = sums[4 * j + 2] + cosine * g_im
                    sums[4 * j + 3] = sums[4 * j + 3] + sine * g_im
        for n in range(4 * half):
            sums_ref[q, delta * 4 * half + n] = sums[n]


def to_offsets(blocks, q, sums_ref, h_ref, back_high_ref, back_low_ref, acc_ref):
    f32 = jnp.float32
    half = LAGS // 2
    chunk = sums_ref.shape[3]
    zero_row = (blocks - 1) * LAGS
    for delta in range(blocks):
        h_re, h_im = [None] * LAGS, [None] * LAGS
        for j in range(half):
            cr, sr, ci, si = [
                jnp.sum(sums_ref[q, (delta * half + j) * 4 + n], axis=0, keepdims=True) for n in range(4)
            ]
            h_re[half + j], h_im[half + j] = cr - si, ci + sr
            h_re[half - 1 - j], h_im[half - 1 - j] = cr + si, ci - sr
        ahead = zero_row + delta * LAGS
        h_ref[pl.ds(ahead, LAGS), pl.ds(0, chunk)] = jnp.concatenate(h_re, axis=0)
        h_ref[pl.ds(ahead, LAGS), pl.ds(chunk, chunk)] = jnp.concatenate(h_im, axis=0)
        if delta > 0:
            behind = zero_row - delta * LAGS
            h_ref[pl.ds(behind, LAGS), pl.ds(0, chunk)] = jnp.concatenate(h_re[::-1], axis=0)
            h_ref[pl.ds(behind, LAGS), pl.ds(chunk, chunk)] = -jnp.concatenate(h_im[::-1], axis=0)
    h_high, h_low = split_rounded(h_ref[...])
    acc_ref[...] += (
        jnp.dot(h_high, back_high_ref[q], preferred_element_type=f32)
        + jnp.dot(h_low, back_high_ref[q], preferred_element_type=f32)
        + jnp.dot(h_high, back_low_ref[q], preferred_element_type=f32)
    )


def stack_kernel(
    blocks,
    mask_ref,
    waves_ref,
    taper_ref,
    raw_hbm,
    table_hbm,
    high_hbm,
    low_hbm,
    back_high_hbm,
    back_low_hbm,
    out_ref,
    raw_ref,
    table_ref,
    high_ref,
    low_ref,
    back_high_ref,
    back_low_ref,
    cast_ref,
    series_ref,
    y_ref,
    spec_ref,
    pre_ref,
    suf_ref,
    all_ref,
    ready_ref,
    white_ref,
    lhs_ref,
    re_ref,
    im_ref,
    sums_ref,
    h_ref,
    acc_ref,
    part_ref,
    got_ref,
    raw_sem,
    table_sem,
    raw_send,
    raw_recv,
    white_send,
    white_recv,
    stack_send,
    stack_recv,
):
    _, n_dev, rows, chans = series_ref.shape
    groups = n_dev // RADIX
    me = own_index()
    f32 = jnp.float32

    def raw_copy(chunk):
        part = pl.ds(pl.multiple_of(chunk * rows, rows), rows)
        return pltpu.make_async_copy(raw_hbm.at[part], raw_ref.at[part], raw_sem.at[chunk])

    def table_copy(n):
        pairs = (
            (table_hbm, table_ref),
            (high_hbm, high_ref),
            (low_hbm, low_ref),
            (back_high_hbm, back_high_ref),
            (back_low_hbm, back_low_ref),
        )
        src, dst = pairs[n]
        return pltpu.make_async_copy(src, dst, table_sem.at[n])

    n_tables = 5

    for chunk in range(RAW_CHUNKS):
        raw_copy(chunk).start()
    greet_all(n_dev)

    def send_raw(chunk):
        part = pl.ds(pl.multiple_of(chunk * rows, rows), rows)
        raw_copy(chunk).wait()
        for other in range(n_dev):
            cast_ref[chunk, other] = raw_ref[part, other * chans : (other + 1) * chans].astype(jnp.bfloat16)

    send_raw(0)
    meet_all(n_dev)
    start_all(n_dev, 0, cast_ref, series_ref, raw_send, raw_recv)

    @pl.loop(1, RAW_CHUNKS)
    def _(chunk):
        send_raw(chunk)
        start_all(n_dev, chunk, cast_ref, series_ref, raw_send, raw_recv)

    for n in range(n_tables):
        table_copy(n).start()
    spec_ref[...] = jnp.zeros_like(spec_ref)
    sums_ref[...] = jnp.zeros_like(sums_ref)
    acc_ref[...] = jnp.zeros_like(acc_ref)
    table_copy(0).wait()

    @pl.loop(0, RAW_CHUNKS)
    def _(chunk):
        series_ref[chunk, me] = cast_ref[chunk, me]
        wait_all(n_dev, chunk, cast_ref, series_ref, raw_send, raw_recv)
        transform(series_ref, chunk, y_ref, spec_ref, table_ref)

    window_sums(spec_ref, pre_ref, suf_ref, all_ref)
    bin_chunks = ready_ref.shape[0]
    per = bin_chunks * BIN_CHUNK

    @pl.loop(0, RADIX)
    def _(i):
        rho = (me // groups + 1 + i) % RADIX
        total = all_ref[...] + suf_ref[rho, pl.ds(PAD - 2, M_ROWS), :] + pre_ref[rho, pl.ds(PAD + 2, M_ROWS), :]
        scale = taper_ref[rho] / (total / (2 * SW + 1) + EPS)
        for part in range(2):
            value = (spec_ref[rho, pl.ds(part * M_ROWS, M_ROWS), :] * scale).astype(jnp.bfloat16)
            for g in range(groups):
                for w in range(bin_chunks):
                    first = g * per + w * BIN_CHUNK
                    ready_ref[w, rho * groups + g, part] = value[first : first + BIN_CHUNK]
        for g in range(groups):
            other = rho * groups + g

            @pl.when(other != me)
            def _():
                slot_copy(ready_ref, white_ref, 0, other, me, white_send, white_recv, other).start()

    @pl.loop(1, bin_chunks)
    def _(w):
        start_all(n_dev, w, ready_ref, white_ref, white_send, white_recv)

    for n in range(1, n_tables):
        table_copy(n).wait()
    per_block = n_dev // blocks
    q_chunks = sums_ref.shape[0]

    @pl.loop(0, bin_chunks)
    def _(w):
        white_ref[w, me] = ready_ref[w, me]
        wait_all(n_dev, w, ready_ref, white_ref, white_send, white_recv)
        for source in range(n_dev):
            block, place = divmod(source, per_block)
            for part in range(2):
                lhs_ref[pl.ds((2 * block + part) * BIN_CHUNK, BIN_CHUNK), pl.ds(place * chans, chans)] = white_ref[
                    w, source, part
                ]

        @pl.loop(0, q_chunks)
        def _(q):
            cross_spectra(
                blocks, w, q, mask_ref, waves_ref, lhs_ref, high_ref, low_ref, re_ref, im_ref, sums_ref
            )

    @pl.loop(0, q_chunks)
    def _(q):
        to_offsets(blocks, q, sums_ref, h_ref, back_high_ref, back_low_ref, acc_ref)

    width = per_block * chans
    cols = part_ref.shape[3]
    parts = width // cols
    for segment in range(2 * blocks):
        value = jnp.zeros((LAGS, width), f32)
        if segment < 2 * blocks - 1:
            value = value + acc_ref[pl.ds(segment * LAGS, LAGS), pl.ds(0, width)]
        if segment > 0:
            value = value + acc_ref[pl.ds((segment - 1) * LAGS, LAGS), pl.ds(width, width)]
        for part in range(parts):
            part_ref[0, segment * parts + part] = value[:, part * cols : (part + 1) * cols]
    start_all(n_dev, 0, part_ref, got_ref, stack_send, stack_recv)
    got_ref[0, me] = part_ref[0, me]
    wait_all(n_dev, 0, part_ref, got_ref, stack_send, stack_recv)
    out_ref[...] = jnp.sum(got_ref[0], axis=0)


def stacked(raw, mask, waves, n_dev):
    samples = raw.shape[0]
    chans = C // n_dev
    blocks = mask.shape[0]
    bins = NB // n_dev
    width = C // blocks
    size = 2 * width
    chunk = LANES
    cols = 2 * C // n_dev
    bin_chunks = bins // BIN_CHUNK
    pairs = RADIX // 2
    f32, b16 = jnp.float32, jnp.bfloat16
    tables = [spectrum_tables(samples), *channel_tables(width, chunk), *offset_tables(width, chunk)]
    rows = (2 * blocks - 1) * LAGS
    whole = pl.BlockSpec(memory_space=pltpu.VMEM)
    away = pl.BlockSpec(memory_space=pl.ANY)
    return pl.pallas_call(
        functools.partial(stack_kernel, blocks),
        out_shape=jax.ShapeDtypeStruct((LAGS, cols), f32),
        in_specs=[pl.BlockSpec(memory_space=pltpu.SMEM), whole, whole] + [away] * 6,
        out_specs=whole,
        scratch_shapes=[
            pltpu.VMEM(raw.shape, f32),
            *[pltpu.VMEM(table.shape, b16) for table in tables],
            pltpu.VMEM((RAW_CHUNKS, n_dev, samples // RAW_CHUNKS, chans), b16),
            pltpu.VMEM((RAW_CHUNKS, n_dev, samples // RAW_CHUNKS, chans), b16),
            pltpu.VMEM((pairs, 2 * SPAN // RAW_CHUNKS, chans), b16),
            pltpu.VMEM((RADIX, 2 * M_ROWS, chans), f32),
            pltpu.VMEM((RADIX, M_ROWS + 2 * PAD, chans), f32),
            pltpu.VMEM((RADIX, M_ROWS + 2 * PAD, chans), f32),
            pltpu.VMEM((M_ROWS, chans), f32),
            pltpu.VMEM((bin_chunks, n_dev, 2, BIN_CHUNK, chans), b16),
            pltpu.VMEM((bin_chunks, n_dev, 2, BIN_CHUNK, chans), b16),
            pltpu.VMEM((blocks * 2 * BIN_CHUNK, width), b16),
            pltpu.VMEM((blocks, BIN_CHUNK, chunk), f32),
            pltpu.VMEM((blocks, BIN_CHUNK, chunk), f32),
            pltpu.VMEM((size // chunk, blocks * 2 * LAGS, 8, chunk), f32),
            pltpu.VMEM((rows, 2 * chunk), f32),
            pltpu.VMEM((rows, size), f32),
            pltpu.VMEM((1, n_dev, LAGS, cols), f32),
            pltpu.VMEM((1, n_dev, LAGS, cols), f32),
            pltpu.SemaphoreType.DMA((RAW_CHUNKS,)),
            pltpu.SemaphoreType.DMA((len(tables),)),
            pltpu.SemaphoreType.DMA((RAW_CHUNKS, n_dev)),
            pltpu.SemaphoreType.DMA((RAW_CHUNKS, n_dev)),
            pltpu.SemaphoreType.DMA((bin_chunks, n_dev)),
            pltpu.SemaphoreType.DMA((bin_chunks, n_dev)),
            pltpu.SemaphoreType.DMA((1, n_dev)),
            pltpu.SemaphoreType.DMA((1, n_dev)),
        ],
        compiler_params=pltpu.CompilerParams(
            vmem_limit_bytes=58 * 2**20, collective_id=0, has_side_effects=True
        ),
        cost_estimate=pl.CostEstimate(flops=6 * 2**30, bytes_accessed=25 * 2**20, transcendentals=0),
        name="stacked",
    )(mask.astype(f32), waves, jnp.asarray(taper_table()), raw, *[jnp.asarray(table) for table in tables])


def lag_waves(device, bins, groups):
    rho, group = device // groups, device % groups
    k = RADIX * (group * bins + lax.iota(jnp.int32, bins) + 1) + rho
    number = lax.iota(jnp.int32, LAGS // 2) + LAGS // 2
    shifts = LAG_STEP * (2 * number + 1 - LAGS) // 2
    phase = jnp.mod(shifts[:, None] * k[None, :], NT).astype(jnp.float32) * (2 * math.pi / NT)
    waves = jnp.concatenate([jnp.cos(phase), jnp.sin(phase)], axis=0)
    return jnp.broadcast_to(waves[:, :, None], (LAGS, bins, LANES))


def pair_counts(mask, columns):
    blocks = mask.shape[0]
    width = C // blocks
    labels = lax.iota(jnp.int32, blocks)
    apart = labels[None, :] - labels[:, None]
    deltas = lax.iota(jnp.int32, 2 * blocks - 1) - (blocks - 1)
    per_delta = jnp.sum(
        mask[None] * (apart[None] == deltas[:, None, None]).astype(jnp.int32), axis=(1, 2)
    )
    offsets = columns - C
    intersection = jnp.maximum(0, width - jnp.abs(offsets[:, None] - width * deltas[None, :]))
    return jnp.sum(intersection * per_delta[None, :], axis=1)


def stack_scale(counts):
    return 1.0 / jnp.sqrt(NB * jnp.maximum(counts, 1).astype(jnp.float32))


def on_device(raw, mask):
    n_dev = lax.axis_size("blk") * lax.axis_size("lag")
    device = own_index()
    waves = lag_waves(device, NB // n_dev, n_dev // RADIX)
    total = stacked(raw, mask, waves, n_dev)
    n_cols = total.shape[1]
    counts = pair_counts(mask, device * n_cols + lax.iota(jnp.int32, n_cols))
    return total * stack_scale(counts)[None, :]


def solution(mesh):
    return jax.shard_map(
        on_device,
        mesh=mesh,
        in_specs=(P(("blk", "lag"), None), P()),
        out_specs=P(None, ("blk", "lag")),
        check_vma=False,
    )
```

```python
import functools
import math

import jax
import jax.numpy as jnp
import ml_dtypes
import numpy as np
from jax import lax
from jax.experimental import pallas as pl
from jax.experimental.pallas import tpu as pltpu
from jax.sharding import PartitionSpec as P

NT = 8192
C = 4096
NB = 2048
K0 = 16
SW = 32
TAPER = 128
LAGS = 8
LAG_STEP = 32
EPS = 1e-06

RADIX = 16
RAW_CHUNKS = 4
BIN_CHUNK = 16
SPAN = NT // RADIX
M_ROWS = NB // RADIX
LANES = 128
PAD = 8
bf16 = ml_dtypes.bfloat16


def split_high_low(table):
    high = table.astype(bf16)
    low = (table - high.astype(np.float64)).astype(bf16)
    return high, low


@functools.cache
def spectrum_tables(samples):
    m = np.arange(M_ROWS)[:, None] + 1
    s = np.arange(SPAN)[None, :]

    def waves(rho):
        angle = 2 * np.pi * (((RADIX * m + rho) * s) % NT) / NT
        return np.cos(angle), np.sin(angle)

    zero = np.zeros((M_ROWS, SPAN))
    tables = []
    c0, s0 = waves(0)
    c8, s8 = waves(RADIX // 2)
    tables.append(np.block([[c0, zero], [-s0, zero], [zero, c8], [zero, -s8]]))
    for rho in range(1, RADIX // 2):
        ca, sa = waves(rho)
        cb, sb = waves(RADIX - rho)
        tables.append(np.block([[ca, sa], [-sa, ca], [cb, -sb], [-sb, -cb]]))
    table = np.stack(tables).astype(bf16)
    rows = samples // RAW_CHUNKS
    shape = (RADIX // 2, 4 * M_ROWS, 2, SPAN // samples, RAW_CHUNKS, rows)
    table = table.reshape(shape).transpose(4, 0, 1, 2, 3, 5)
    return table.reshape(RAW_CHUNKS, RADIX // 2, 4 * M_ROWS, 2 * SPAN // RAW_CHUNKS)


@functools.cache
def taper_table():
    j = np.arange(NB, dtype=np.float64)
    edge = np.minimum(j, NB - 1 - j)
    weights = np.where(edge < TAPER, 0.5 - 0.5 * np.cos(math.pi * (edge + 0.5) / TAPER), 1.0)
    weights = weights.reshape(M_ROWS, RADIX).T
    return np.ascontiguousarray(weights.astype(np.float32)[:, :, None])


@functools.cache
def channel_tables(width, chunk):
    size = 2 * width
    c = np.arange(width)[:, None]
    q = np.arange(size)[None, :]
    angle = 2 * np.pi * ((c * q) % size) / size
    both = np.stack([np.cos(angle), np.sin(angle)], axis=1).reshape(width, 2, size // chunk, chunk)
    both = both.transpose(2, 0, 1, 3).reshape(size // chunk, width, 2 * chunk)
    return split_high_low(both)


@functools.cache
def offset_tables(width, chunk):
    size = 2 * width
    q = np.arange(size)[:, None]
    d = np.arange(size)[None, :] - width
    angle = 2 * np.pi * ((q * d) % size) / size
    both = np.stack([np.cos(angle), np.sin(angle)]) / size
    both[:, :, 0] = 0.0
    both = both.reshape(2, size // chunk, chunk, size).transpose(1, 0, 2, 3)
    return split_high_low(both.reshape(size // chunk, 2 * chunk, size))


@functools.cache
def lag_waves(n_dev):
    groups = n_dev // RADIX
    bins = NB // n_dev
    device = np.arange(n_dev)[:, None]
    k = RADIX * ((device % groups) * bins + np.arange(bins)[None, :] + 1) + device // groups
    number = np.arange(LAGS // 2) + LAGS // 2
    shifts = LAG_STEP * (2 * number + 1 - LAGS) // 2
    phase = 2 * np.pi * ((shifts[None, :, None] * k[:, None, :]) % NT) / NT
    waves = np.concatenate([np.cos(phase), np.sin(phase)], axis=1).astype(np.float32)
    return np.ascontiguousarray(np.broadcast_to(waves[..., None], (*waves.shape, LANES)))


def real_dft16(x):
    a = [x[h] + x[h + 8] for h in range(8)]
    b = [x[h] - x[h + 8] for h in range(8)]
    out = {}
    lo = [a[h] + a[h + 4] for h in range(4)]
    d = [a[h] - a[h + 4] for h in range(4)]
    out[0] = (lo[0] + lo[2]) + (lo[1] + lo[3])
    out[8] = (lo[0] + lo[2]) - (lo[1] + lo[3])
    out[4] = (lo[0] - lo[2], lo[3] - lo[1])
    root = math.sqrt(0.5)
    minus, plus = (d[1] - d[3]) * root, (d[1] + d[3]) * root
    out[2] = (d[0] + minus, -(d[2] + plus))
    out[6] = (d[0] - minus, d[2] - plus)
    diff = [None] + [b[h] - b[8 - h] for h in range(1, 4)]
    add = [None] + [b[h] + b[8 - h] for h in range(1, 4)]
    for rho in (1, 3, 5, 7):
        re, im = b[0], b[4] * (-math.sin(math.pi * rho / 2))
        for h in range(1, 4):
            re = re + diff[h] * math.cos(math.pi * h * rho / 8)
            im = im - add[h] * math.sin(math.pi * h * rho / 8)
        out[rho] = (re, im)
    return out


def own_index():
    return lax.axis_index("blk") * lax.axis_size("lag") + lax.axis_index("lag")


def coordinates(device):
    n_lag = lax.axis_size("lag")
    return (device // n_lag, device % n_lag)


def greet_all(n_dev):
    barrier = pltpu.get_barrier_semaphore()
    me = own_index()

    @pl.loop(1, n_dev)
    def _(ahead):
        other = (me + ahead) % n_dev
        pl.semaphore_signal(barrier, inc=1, device_id=coordinates(other), device_id_type=pl.DeviceIdType.MESH)


def meet_all(n_dev):
    pl.semaphore_wait(pltpu.get_barrier_semaphore(), n_dev - 1)


def split_rounded(value):
    high = value.astype(jnp.bfloat16)
    return high, (value - high.astype(jnp.float32)).astype(jnp.bfloat16)


def slot_copy(src_ref, dst_ref, chunk, src, dst, send_sem, recv_sem, device):
    return pltpu.make_async_remote_copy(
        src_ref=src_ref.at[chunk, src],
        dst_ref=dst_ref.at[chunk, dst],
        send_sem=send_sem.at[chunk, src],
        recv_sem=recv_sem.at[chunk, dst],
        device_id=coordinates(device),
        device_id_type=pl.DeviceIdType.MESH,
    )


def start_all(n_dev, chunk, src_ref, dst_ref, send_sem, recv_sem):
    me = own_index()

    @pl.loop(1, n_dev)
    def _(ahead):
        other = (me + ahead) % n_dev
        slot_copy(src_ref, dst_ref, chunk, other, me, send_sem, recv_sem, other).start()


def wait_all(n_dev, chunk, src_ref, dst_ref, send_sem, recv_sem):
    me = own_index()

    @pl.loop(1, n_dev)
    def _(ahead):
        other = (me + ahead) % n_dev
        slot_copy(src_ref, dst_ref, chunk, other, other, send_sem, recv_sem, other).wait_recv()


def wait_sent(n_dev, chunk, src_ref, dst_ref, send_sem, recv_sem):
    me = own_index()

    @pl.loop(1, n_dev)
    def _(ahead):
        other = (me + ahead) % n_dev
        slot_copy(src_ref, dst_ref, chunk, other, other, send_sem, recv_sem, other).wait_send()


def sum_along(axis, src_ref, got_ref, send_sem, recv_sem, meanwhile):
    size = lax.axis_size(axis)
    me = lax.axis_index(axis)

    def copy(src, dst, device):
        return pltpu.make_async_remote_copy(
            src_ref=src_ref.at[src],
            dst_ref=got_ref.at[dst],
            send_sem=send_sem.at[src],
            recv_sem=recv_sem.at[dst],
            device_id={axis: device},
            device_id_type=pl.DeviceIdType.MESH,
        )

    @pl.loop(1, size)
    def _(ahead):
        other = (me + ahead) % size
        copy(other, me, other).start()

    got_ref[me] = src_ref[me]
    meanwhile()

    @pl.loop(1, size)
    def _(ahead):
        other = (me + ahead) % size
        copy(other, other, other).wait_recv()

    @pl.loop(1, size)
    def _(ahead):
        other = (me + ahead) % size
        copy(other, other, other).wait_send()

    return jnp.sum(got_ref[...], axis=0)


def transform(series_ref, chunk, y_ref, spec_ref, table_ref):
    half = RADIX // 2
    tile = 16
    _, n_dev, rows, _ = series_ref.shape
    pieces = n_dev // RADIX
    span = pieces * rows
    per_piece = rows // tile

    @pl.loop(0, span // tile)
    def _(i):
        start = pl.multiple_of(i * tile, tile)
        inside = pl.multiple_of((i % per_piece) * tile, tile)
        x = [
            series_ref[chunk, h * pieces + i // per_piece, pl.ds(inside, tile), :].astype(jnp.float32)
            for h in range(RADIX)
        ]
        y = real_dft16(x)
        y[0] = (y[0], y[half])
        for rho in range(half):
            for part in range(2):
                y_ref[rho, pl.ds(part * span + start, tile), :] = y[rho][part].astype(jnp.bfloat16)

    @pl.loop(0, half)
    def _(pair):
        both = jnp.dot(table_ref[chunk, pair], y_ref[pair], preferred_element_type=jnp.float32)
        other = jnp.where(pair == 0, half, RADIX - pair)
        spec_ref[pair] += both[: 2 * M_ROWS]
        spec_ref[other] += both[2 * M_ROWS :]


def window_sums(spec_ref, pre_ref, suf_ref, all_ref):
    edge = jnp.zeros((PAD, all_ref.shape[1]), jnp.float32)
    inner = pl.ds(PAD, M_ROWS)
    for rho in range(RADIX):
        re = spec_ref[rho, pl.ds(0, M_ROWS), :]
        im = spec_ref[rho, pl.ds(M_ROWS, M_ROWS), :]
        amp = jnp.sqrt(re * re + im * im)
        suf_ref[rho, inner, :] = amp
        pre_ref[rho, inner, :] = amp if rho == 0 else pre_ref[rho - 1, inner, :] + amp
        for ref in (pre_ref, suf_ref):
            ref[rho, pl.ds(0, PAD), :] = edge
            ref[rho, pl.ds(PAD + M_ROWS, PAD), :] = edge
    for rho in range(RADIX - 2, -1, -1):
        suf_ref[rho, inner, :] = suf_ref[rho, inner, :] + suf_ref[rho + 1, inner, :]
    last = RADIX - 1
    all_ref[...] = (
        pre_ref[last, pl.ds(PAD - 1, M_ROWS), :]
        + pre_ref[last, inner, :]
        + pre_ref[last, pl.ds(PAD + 1, M_ROWS), :]
    )


def cross_spectra(blocks, bin_chunk, q, mask_ref, waves_ref, lhs_ref, high_ref, low_ref, re_ref, im_ref, sums_ref):
    f32 = jnp.float32
    half = LAGS // 2
    chunk = re_ref.shape[2]
    bins = BIN_CHUNK
    lhs = lhs_ref[...]
    product = jnp.dot(lhs, high_ref[q], preferred_element_type=f32)
    product = product + jnp.dot(lhs, low_ref[q], preferred_element_type=f32)
    for block in range(blocks):
        real = product[2 * block * bins : (2 * block + 1) * bins]
        imag = product[(2 * block + 1) * bins : (2 * block + 2) * bins]
        re_ref[block] = real[:, :chunk] + imag[:, chunk:]
        im_ref[block] = imag[:, :chunk] - real[:, chunk:]
    for delta in range(blocks):
        sums = [sums_ref[q, delta * 4 * half + n] for n in range(4 * half)]
        for b in range(bins // 8):
            rows = pl.ds(8 * b, 8)
            wave_rows = pl.ds(pl.multiple_of(bin_chunk * bins + 8 * b, 8), 8)
            g_re = jnp.zeros((8, chunk), f32)
            g_im = jnp.zeros((8, chunk), f32)
            for block in range(blocks - delta):
                keep = mask_ref[block, block + delta].astype(f32)
                a_re, a_im = re_ref[block, rows, :], im_ref[block, rows, :]
                if delta == 0:
                    g_re = g_re + keep * (a_re * a_re + a_im * a_im)
                else:
                    b_re, b_im = re_ref[block + delta, rows, :], im_ref[block + delta, rows, :]
                    g_re = g_re + keep * (a_re * b_re + a_im * b_im)
                    g_im = g_im + keep * (a_im * b_re - a_re * b_im)
            for j in range(half):
                cosine, sine = waves_ref[j, wave_rows, :], waves_ref[half + j, wave_rows, :]
                sums[4 * j] = sums[4 * j] + cosine * g_re
                sums[4 * j + 1] = sums[4 * j + 1] + sine * g_re
                if delta > 0:
                    sums[4 * j + 2] = sums[4 * j + 2] + cosine * g_im
                    sums[4 * j + 3] = sums[4 * j + 3] + sine * g_im
        for n in range(4 * half):
            sums_ref[q, delta * 4 * half + n] = sums[n]


def to_offsets(blocks, q, sums_ref, h_ref, back_high_ref, back_low_ref, acc_ref):
    f32 = jnp.float32
    half = LAGS // 2
    chunk = sums_ref.shape[3]
    zero_row = (blocks - 1) * LAGS
    for delta in range(blocks):
        h_re, h_im = [None] * LAGS, [None] * LAGS
        for j in range(half):
            cr, sr, ci, si = [
                jnp.sum(sums_ref[q, (delta * half + j) * 4 + n], axis=0, keepdims=True) for n in range(4)
            ]
            h_re[half + j], h_im[half + j] = cr - si, ci + sr
            h_re[half - 1 - j], h_im[half - 1 - j] = cr + si, ci - sr
        ahead = zero_row + delta * LAGS
        h_ref[pl.ds(ahead, LAGS), pl.ds(0, chunk)] = jnp.concatenate(h_re, axis=0)
        h_ref[pl.ds(ahead, LAGS), pl.ds(chunk, chunk)] = jnp.concatenate(h_im, axis=0)
        if delta > 0:
            behind = zero_row - delta * LAGS
            h_ref[pl.ds(behind, LAGS), pl.ds(0, chunk)] = jnp.concatenate(h_re[::-1], axis=0)
            h_ref[pl.ds(behind, LAGS), pl.ds(chunk, chunk)] = -jnp.concatenate(h_im[::-1], axis=0)
    h_high, h_low = split_rounded(h_ref[...])
    acc_ref[...] += (
        jnp.dot(h_high, back_high_ref[q], preferred_element_type=f32)
        + jnp.dot(h_low, back_high_ref[q], preferred_element_type=f32)
        + jnp.dot(h_high, back_low_ref[q], preferred_element_type=f32)
    )


def stack_kernel(
    blocks,
    mask_ref,
    taper_ref,
    waves_hbm,
    raw_hbm,
    table_hbm,
    high_hbm,
    low_hbm,
    back_high_hbm,
    back_low_hbm,
    out_ref,
    waves_ref,
    raw_ref,
    table_ref,
    high_ref,
    low_ref,
    back_high_ref,
    back_low_ref,
    cast_ref,
    series_ref,
    y_ref,
    spec_ref,
    pre_ref,
    suf_ref,
    all_ref,
    ready_ref,
    white_ref,
    lhs_ref,
    re_ref,
    im_ref,
    sums_ref,
    h_ref,
    acc_ref,
    part_ref,
    got_ref,
    plane_ref,
    plane_got_ref,
    raw_sem,
    table_sem,
    raw_send,
    raw_recv,
    white_send,
    white_recv,
    stack_send,
    stack_recv,
    plane_send,
    plane_recv,
):
    _, n_dev, rows, chans = series_ref.shape
    groups = n_dev // RADIX
    me = own_index()
    f32 = jnp.float32

    def raw_copy(chunk):
        part = pl.ds(pl.multiple_of(chunk * rows, rows), rows)
        return pltpu.make_async_copy(raw_hbm.at[part], raw_ref.at[part], raw_sem.at[chunk])

    def table_copy(n):
        pairs = (
            (table_hbm, table_ref),
            (high_hbm, high_ref),
            (low_hbm, low_ref),
            (back_high_hbm, back_high_ref),
            (back_low_hbm, back_low_ref),
            (waves_hbm.at[me], waves_ref),
        )
        src, dst = pairs[n]
        return pltpu.make_async_copy(src, dst, table_sem.at[n])

    n_tables = 6

    for chunk in range(RAW_CHUNKS):
        raw_copy(chunk).start()
    greet_all(n_dev)

    def send_raw(chunk):
        part = pl.ds(pl.multiple_of(chunk * rows, rows), rows)
        raw_copy(chunk).wait()
        for other in range(n_dev):
            cast_ref[chunk, other] = raw_ref[part, other * chans : (other + 1) * chans].astype(jnp.bfloat16)

    send_raw(0)
    meet_all(n_dev)
    start_all(n_dev, 0, cast_ref, series_ref, raw_send, raw_recv)

    @pl.loop(1, RAW_CHUNKS)
    def _(chunk):
        send_raw(chunk)
        start_all(n_dev, chunk, cast_ref, series_ref, raw_send, raw_recv)

    for n in range(n_tables):
        table_copy(n).start()
    spec_ref[...] = jnp.zeros_like(spec_ref)
    sums_ref[...] = jnp.zeros_like(sums_ref)
    acc_ref[...] = jnp.zeros_like(acc_ref)
    table_copy(0).wait()

    @pl.loop(0, RAW_CHUNKS)
    def _(chunk):
        series_ref[chunk, me] = cast_ref[chunk, me]
        wait_all(n_dev, chunk, cast_ref, series_ref, raw_send, raw_recv)
        transform(series_ref, chunk, y_ref, spec_ref, table_ref)

    window_sums(spec_ref, pre_ref, suf_ref, all_ref)
    bin_chunks = ready_ref.shape[0]
    per = bin_chunks * BIN_CHUNK

    @pl.loop(0, RADIX)
    def _(i):
        rho = (me // groups + 1 + i) % RADIX
        total = all_ref[...] + suf_ref[rho, pl.ds(PAD - 2, M_ROWS), :] + pre_ref[rho, pl.ds(PAD + 2, M_ROWS), :]
        scale = taper_ref[rho] / (total / (2 * SW + 1) + EPS)
        for part in range(2):
            value = (spec_ref[rho, pl.ds(part * M_ROWS, M_ROWS), :] * scale).astype(jnp.bfloat16)
            for g in range(groups):
                for w in range(bin_chunks):
                    first = g * per + w * BIN_CHUNK
                    ready_ref[w, rho * groups + g, part] = value[first : first + BIN_CHUNK]
        for g in range(groups):
            other = rho * groups + g

            @pl.when(other != me)
            def _():
                slot_copy(ready_ref, white_ref, 0, other, me, white_send, white_recv, other).start()

    @pl.loop(1, bin_chunks)
    def _(w):
        start_all(n_dev, w, ready_ref, white_ref, white_send, white_recv)

    @pl.loop(0, RAW_CHUNKS)
    def _(chunk):
        wait_sent(n_dev, chunk, cast_ref, series_ref, raw_send, raw_recv)

    for n in range(1, n_tables):
        table_copy(n).wait()
    per_block = n_dev // blocks
    q_chunks = sums_ref.shape[0]

    @pl.loop(0, bin_chunks)
    def _(w):
        white_ref[w, me] = ready_ref[w, me]
        wait_all(n_dev, w, ready_ref, white_ref, white_send, white_recv)
        for source in range(n_dev):
            block, place = divmod(source, per_block)
            for part in range(2):
                lhs_ref[pl.ds((2 * block + part) * BIN_CHUNK, BIN_CHUNK), pl.ds(place * chans, chans)] = white_ref[
                    w, source, part
                ]

        @pl.loop(0, q_chunks)
        def _(q):
            cross_spectra(
                blocks, w, q, mask_ref, waves_ref, lhs_ref, high_ref, low_ref, re_ref, im_ref, sums_ref
            )

    @pl.loop(0, q_chunks)
    def _(q):
        to_offsets(blocks, q, sums_ref, h_ref, back_high_ref, back_low_ref, acc_ref)

    width = per_block * chans
    n_blk, n_lag, _, cols = part_ref.shape
    parts = width // cols
    for segment in range(2 * blocks):
        value = jnp.zeros((LAGS, width), f32)
        if segment < 2 * blocks - 1:
            value = value + acc_ref[pl.ds(segment * LAGS, LAGS), pl.ds(0, width)]
        if segment > 0:
            value = value + acc_ref[pl.ds((segment - 1) * LAGS, LAGS), pl.ds(width, width)]
        for part in range(parts):
            part_ref[*divmod(segment * parts + part, n_lag)] = value[:, part * cols : (part + 1) * cols]

    def finish_white():
        @pl.loop(0, bin_chunks)
        def _(w):
            wait_sent(n_dev, w, ready_ref, white_ref, white_send, white_recv)

    plane_ref[...] = sum_along("blk", part_ref, got_ref, stack_send, stack_recv, finish_white)
    out_ref[...] = sum_along("lag", plane_ref, plane_got_ref, plane_send, plane_recv, lambda: None)


def stacked(raw, mask, n_dev):
    samples = raw.shape[0]
    chans = C // n_dev
    blocks = mask.shape[0]
    bins = NB // n_dev
    width = C // blocks
    size = 2 * width
    chunk = LANES
    cols = 2 * C // n_dev
    n_blk, n_lag = lax.axis_size("blk"), lax.axis_size("lag")
    waves = lag_waves(n_dev)
    bin_chunks = bins // BIN_CHUNK
    pairs = RADIX // 2
    f32, b16 = jnp.float32, jnp.bfloat16
    tables = [spectrum_tables(samples), *channel_tables(width, chunk), *offset_tables(width, chunk)]
    rows = (2 * blocks - 1) * LAGS
    whole = pl.BlockSpec(memory_space=pltpu.VMEM)
    away = pl.BlockSpec(memory_space=pl.ANY)
    return pl.pallas_call(
        functools.partial(stack_kernel, blocks),
        out_shape=jax.ShapeDtypeStruct((LAGS, cols), f32),
        in_specs=[pl.BlockSpec(memory_space=pltpu.SMEM), whole] + [away] * 7,
        out_specs=whole,
        scratch_shapes=[
            pltpu.VMEM(waves.shape[1:], f32),
            pltpu.VMEM(raw.shape, f32),
            *[pltpu.VMEM(table.shape, b16) for table in tables],
            pltpu.VMEM((RAW_CHUNKS, n_dev, samples // RAW_CHUNKS, chans), b16),
            pltpu.VMEM((RAW_CHUNKS, n_dev, samples // RAW_CHUNKS, chans), b16),
            pltpu.VMEM((pairs, 2 * SPAN // RAW_CHUNKS, chans), b16),
            pltpu.VMEM((RADIX, 2 * M_ROWS, chans), f32),
            pltpu.VMEM((RADIX, M_ROWS + 2 * PAD, chans), f32),
            pltpu.VMEM((RADIX, M_ROWS + 2 * PAD, chans), f32),
            pltpu.VMEM((M_ROWS, chans), f32),
            pltpu.VMEM((bin_chunks, n_dev, 2, BIN_CHUNK, chans), b16),
            pltpu.VMEM((bin_chunks, n_dev, 2, BIN_CHUNK, chans), b16),
            pltpu.VMEM((blocks * 2 * BIN_CHUNK, width), b16),
            pltpu.VMEM((blocks, BIN_CHUNK, chunk), f32),
            pltpu.VMEM((blocks, BIN_CHUNK, chunk), f32),
            pltpu.VMEM((size // chunk, blocks * 2 * LAGS, 8, chunk), f32),
            pltpu.VMEM((rows, 2 * chunk), f32),
            pltpu.VMEM((rows, size), f32),
            pltpu.VMEM((n_blk, n_lag, LAGS, cols), f32),
            pltpu.VMEM((n_blk, n_lag, LAGS, cols), f32),
            pltpu.VMEM((n_lag, LAGS, cols), f32),
            pltpu.VMEM((n_lag, LAGS, cols), f32),
            pltpu.SemaphoreType.DMA((RAW_CHUNKS,)),
            pltpu.SemaphoreType.DMA((len(tables) + 1,)),
            pltpu.SemaphoreType.DMA((RAW_CHUNKS, n_dev)),
            pltpu.SemaphoreType.DMA((RAW_CHUNKS, n_dev)),
            pltpu.SemaphoreType.DMA((bin_chunks, n_dev)),
            pltpu.SemaphoreType.DMA((bin_chunks, n_dev)),
            pltpu.SemaphoreType.DMA((n_blk,)),
            pltpu.SemaphoreType.DMA((n_blk,)),
            pltpu.SemaphoreType.DMA((n_lag,)),
            pltpu.SemaphoreType.DMA((n_lag,)),
        ],
        compiler_params=pltpu.CompilerParams(
            vmem_limit_bytes=58 * 2**20, collective_id=0, has_side_effects=True
        ),
        cost_estimate=pl.CostEstimate(flops=6 * 2**30, bytes_accessed=25 * 2**20, transcendentals=0),
        name="stacked",
    )(mask, jnp.asarray(taper_table()), jnp.asarray(waves), raw, *[jnp.asarray(table) for table in tables])


def pair_counts(mask, columns):
    blocks = mask.shape[0]
    width = C // blocks
    labels = lax.iota(jnp.int32, blocks)
    apart = labels[None, :] - labels[:, None]
    deltas = lax.iota(jnp.int32, 2 * blocks - 1) - (blocks - 1)
    per_delta = jnp.sum(
        mask[None] * (apart[None] == deltas[:, None, None]).astype(jnp.int32), axis=(1, 2)
    )
    offsets = columns - C
    intersection = jnp.maximum(0, width - jnp.abs(offsets[:, None] - width * deltas[None, :]))
    return jnp.sum(intersection * per_delta[None, :], axis=1)


def stack_scale(counts):
    return 1.0 / jnp.sqrt(NB * jnp.maximum(counts, 1).astype(jnp.float32))


def on_device(raw, mask):
    n_dev = lax.axis_size("blk") * lax.axis_size("lag")
    device = own_index()
    total = stacked(raw, mask, n_dev)
    n_cols = total.shape[1]
    counts = pair_counts(mask, device * n_cols + lax.iota(jnp.int32, n_cols))
    return total * stack_scale(counts)[None, :]


def solution(mesh):
    return jax.shard_map(
        on_device,
        mesh=mesh,
        in_specs=(P(("blk", "lag"), None), P()),
        out_specs=P(None, ("blk", "lag")),
        check_vma=False,
    )
```

```python
import functools
import math

import jax
import jax.numpy as jnp
import ml_dtypes
import numpy as np
from jax import lax
from jax.experimental import pallas as pl
from jax.experimental.pallas import tpu as pltpu
from jax.sharding import PartitionSpec as P

NT = 8192
C = 4096
NB = 2048
K0 = 16
SW = 32
TAPER = 128
LAGS = 8
LAG_STEP = 32
EPS = 1e-06

RADIX = 16
RAW_CHUNKS = 4
BIN_CHUNK = 16
SPAN = NT // RADIX
M_ROWS = NB // RADIX
LANES = 128
PAD = 8
bf16 = ml_dtypes.bfloat16


def split_high_low(table):
    high = table.astype(bf16)
    low = (table - high.astype(np.float64)).astype(bf16)
    return high, low


@functools.cache
def spectrum_tables(samples):
    m = np.arange(M_ROWS)[:, None] + 1
    s = np.arange(SPAN)[None, :]

    def waves(rho):
        angle = 2 * np.pi * (((RADIX * m + rho) * s) % NT) / NT
        return np.cos(angle), np.sin(angle)

    zero = np.zeros((M_ROWS, SPAN))
    tables = []
    c0, s0 = waves(0)
    c8, s8 = waves(RADIX // 2)
    tables.append(np.block([[c0, zero], [-s0, zero], [zero, c8], [zero, -s8]]))
    for rho in range(1, RADIX // 2):
        ca, sa = waves(rho)
        cb, sb = waves(RADIX - rho)
        tables.append(np.block([[ca, sa], [-sa, ca], [cb, -sb], [-sb, -cb]]))
    table = np.stack(tables).astype(bf16)
    rows = samples // RAW_CHUNKS
    shape = (RADIX // 2, 4 * M_ROWS, 2, SPAN // samples, RAW_CHUNKS, rows)
    table = table.reshape(shape).transpose(4, 0, 1, 2, 3, 5)
    return table.reshape(RAW_CHUNKS, RADIX // 2, 4 * M_ROWS, 2 * SPAN // RAW_CHUNKS)


@functools.cache
def taper_table():
    j = np.arange(NB, dtype=np.float64)
    edge = np.minimum(j, NB - 1 - j)
    weights = np.where(edge < TAPER, 0.5 - 0.5 * np.cos(math.pi * (edge + 0.5) / TAPER), 1.0)
    weights = weights.reshape(M_ROWS, RADIX).T
    return np.ascontiguousarray(weights.astype(np.float32)[:, :, None])


@functools.cache
def channel_tables(width, chunk):
    size = 2 * width
    c = np.arange(width)[:, None]
    q = np.arange(size)[None, :]
    angle = 2 * np.pi * ((c * q) % size) / size
    both = np.stack([np.cos(angle), np.sin(angle)], axis=1).reshape(width, 2, size // chunk, chunk)
    both = both.transpose(2, 0, 1, 3).reshape(size // chunk, width, 2 * chunk)
    return split_high_low(both)


@functools.cache
def offset_tables(width, chunk):
    size = 2 * width
    q = np.arange(size)[:, None]
    d = np.arange(size)[None, :] - width
    angle = 2 * np.pi * ((q * d) % size) / size
    both = np.stack([np.cos(angle), np.sin(angle)]) / size
    both[:, :, 0] = 0.0
    both = both.reshape(2, size // chunk, chunk, size).transpose(1, 0, 2, 3)
    return split_high_low(both.reshape(size // chunk, 2 * chunk, size))


@functools.cache
def lag_waves(n_dev):
    groups = n_dev // RADIX
    bins = NB // n_dev
    device = np.arange(n_dev)[:, None]
    k = RADIX * ((device % groups) * bins + np.arange(bins)[None, :] + 1) + device // groups
    number = np.arange(LAGS // 2) + LAGS // 2
    shifts = LAG_STEP * (2 * number + 1 - LAGS) // 2
    phase = 2 * np.pi * ((shifts[None, :, None] * k[:, None, :]) % NT) / NT
    waves = np.concatenate([np.cos(phase), np.sin(phase)], axis=1).astype(np.float32)
    return np.ascontiguousarray(np.broadcast_to(waves[..., None], (*waves.shape, LANES)))


def real_dft16(x):
    a = [x[h] + x[h + 8] for h in range(8)]
    b = [x[h] - x[h + 8] for h in range(8)]
    out = {}
    lo = [a[h] + a[h + 4] for h in range(4)]
    d = [a[h] - a[h + 4] for h in range(4)]
    out[0] = (lo[0] + lo[2]) + (lo[1] + lo[3])
    out[8] = (lo[0] + lo[2]) - (lo[1] + lo[3])
    out[4] = (lo[0] - lo[2], lo[3] - lo[1])
    root = math.sqrt(0.5)
    minus, plus = (d[1] - d[3]) * root, (d[1] + d[3]) * root
    out[2] = (d[0] + minus, -(d[2] + plus))
    out[6] = (d[0] - minus, d[2] - plus)
    diff = [None] + [b[h] - b[8 - h] for h in range(1, 4)]
    add = [None] + [b[h] + b[8 - h] for h in range(1, 4)]
    for rho in (1, 3, 5, 7):
        re, im = b[0], b[4] * (-math.sin(math.pi * rho / 2))
        for h in range(1, 4):
            re = re + diff[h] * math.cos(math.pi * h * rho / 8)
            im = im - add[h] * math.sin(math.pi * h * rho / 8)
        out[rho] = (re, im)
    return out


def own_index():
    return lax.axis_index("blk") * lax.axis_size("lag") + lax.axis_index("lag")


def coordinates(device):
    n_lag = lax.axis_size("lag")
    return (device // n_lag, device % n_lag)


def greet_all(n_dev):
    barrier = pltpu.get_barrier_semaphore()
    me = own_index()

    @pl.loop(1, n_dev)
    def _(ahead):
        other = (me + ahead) % n_dev
        pl.semaphore_signal(barrier, inc=1, device_id=coordinates(other), device_id_type=pl.DeviceIdType.MESH)


def meet_all(n_dev):
    pl.semaphore_wait(pltpu.get_barrier_semaphore(), n_dev - 1)


def split_rounded(value):
    high = value.astype(jnp.bfloat16)
    return high, (value - high.astype(jnp.float32)).astype(jnp.bfloat16)


def slot_copy(src_ref, dst_ref, chunk, src, dst, send_sem, recv_sem, device):
    return pltpu.make_async_remote_copy(
        src_ref=src_ref.at[chunk, src],
        dst_ref=dst_ref.at[chunk, dst],
        send_sem=send_sem.at[chunk, src],
        recv_sem=recv_sem.at[chunk, dst],
        device_id=coordinates(device),
        device_id_type=pl.DeviceIdType.MESH,
    )


def start_all(n_dev, chunk, src_ref, dst_ref, send_sem, recv_sem):
    me = own_index()

    @pl.loop(1, n_dev)
    def _(ahead):
        other = (me + ahead) % n_dev
        slot_copy(src_ref, dst_ref, chunk, other, me, send_sem, recv_sem, other).start()


def wait_all(n_dev, chunk, src_ref, dst_ref, send_sem, recv_sem):
    me = own_index()

    @pl.loop(1, n_dev)
    def _(ahead):
        other = (me + ahead) % n_dev
        slot_copy(src_ref, dst_ref, chunk, other, other, send_sem, recv_sem, other).wait_recv()


def wait_sent(n_dev, chunk, src_ref, dst_ref, send_sem, recv_sem):
    me = own_index()

    @pl.loop(1, n_dev)
    def _(ahead):
        other = (me + ahead) % n_dev
        slot_copy(src_ref, dst_ref, chunk, other, other, send_sem, recv_sem, other).wait_send()


def sum_along(axis, src_ref, got_ref, send_sem, recv_sem):
    size = lax.axis_size(axis)
    me = lax.axis_index(axis)

    def copy(src, dst, device):
        return pltpu.make_async_remote_copy(
            src_ref=src_ref.at[src],
            dst_ref=got_ref.at[dst],
            send_sem=send_sem.at[src],
            recv_sem=recv_sem.at[dst],
            device_id={axis: device},
            device_id_type=pl.DeviceIdType.MESH,
        )

    @pl.loop(1, size)
    def _(ahead):
        other = (me + ahead) % size
        copy(other, me, other).start()

    got_ref[me] = src_ref[me]

    @pl.loop(1, size)
    def _(ahead):
        other = (me + ahead) % size
        copy(other, other, other).wait_recv()

    @pl.loop(1, size)
    def _(ahead):
        other = (me + ahead) % size
        copy(other, other, other).wait_send()

    return jnp.sum(got_ref[...], axis=0)


def transform(series_ref, chunk, y_ref, spec_ref, table_ref):
    half = RADIX // 2
    tile = 16
    _, n_dev, rows, _ = series_ref.shape
    pieces = n_dev // RADIX
    span = pieces * rows
    per_piece = rows // tile

    @pl.loop(0, span // tile)
    def _(i):
        start = pl.multiple_of(i * tile, tile)
        inside = pl.multiple_of((i % per_piece) * tile, tile)
        x = [
            series_ref[chunk, h * pieces + i // per_piece, pl.ds(inside, tile), :].astype(jnp.float32)
            for h in range(RADIX)
        ]
        y = real_dft16(x)
        y[0] = (y[0], y[half])
        for rho in range(half):
            for part in range(2):
                y_ref[rho, pl.ds(part * span + start, tile), :] = y[rho][part].astype(jnp.bfloat16)

    @pl.loop(0, half)
    def _(pair):
        both = jnp.dot(table_ref[chunk, pair], y_ref[pair], preferred_element_type=jnp.float32)
        other = jnp.where(pair == 0, half, RADIX - pair)
        spec_ref[pair] += both[: 2 * M_ROWS]
        spec_ref[other] += both[2 * M_ROWS :]


def window_sums(spec_ref, pre_ref, suf_ref, all_ref):
    edge = jnp.zeros((PAD, all_ref.shape[1]), jnp.float32)
    inner = pl.ds(PAD, M_ROWS)
    for rho in range(RADIX):
        re = spec_ref[rho, pl.ds(0, M_ROWS), :]
        im = spec_ref[rho, pl.ds(M_ROWS, M_ROWS), :]
        amp = jnp.sqrt(re * re + im * im)
        suf_ref[rho, inner, :] = amp
        pre_ref[rho, inner, :] = amp if rho == 0 else pre_ref[rho - 1, inner, :] + amp
        for ref in (pre_ref, suf_ref):
            ref[rho, pl.ds(0, PAD), :] = edge
            ref[rho, pl.ds(PAD + M_ROWS, PAD), :] = edge
    for rho in range(RADIX - 2, -1, -1):
        suf_ref[rho, inner, :] = suf_ref[rho, inner, :] + suf_ref[rho + 1, inner, :]
    last = RADIX - 1
    all_ref[...] = (
        pre_ref[last, pl.ds(PAD - 1, M_ROWS), :]
        + pre_ref[last, inner, :]
        + pre_ref[last, pl.ds(PAD + 1, M_ROWS), :]
    )


def cross_spectra(blocks, bin_chunk, q, mask_ref, waves_ref, lhs_ref, high_ref, low_ref, re_ref, im_ref, sums_ref):
    f32 = jnp.float32
    half = LAGS // 2
    chunk = re_ref.shape[2]
    bins = BIN_CHUNK
    lhs = lhs_ref[...]
    product = jnp.dot(lhs, high_ref[q], preferred_element_type=f32)
    product = product + jnp.dot(lhs, low_ref[q], preferred_element_type=f32)
    for block in range(blocks):
        real = product[2 * block * bins : (2 * block + 1) * bins]
        imag = product[(2 * block + 1) * bins : (2 * block + 2) * bins]
        re_ref[block] = real[:, :chunk] + imag[:, chunk:]
        im_ref[block] = imag[:, :chunk] - real[:, chunk:]
    for delta in range(blocks):
        sums = [sums_ref[q, delta * 4 * half + n] for n in range(4 * half)]
        for b in range(bins // 8):
            rows = pl.ds(8 * b, 8)
            wave_rows = pl.ds(pl.multiple_of(bin_chunk * bins + 8 * b, 8), 8)
            g_re = jnp.zeros((8, chunk), f32)
            g_im = jnp.zeros((8, chunk), f32)
            for block in range(blocks - delta):
                keep = mask_ref[block, block + delta].astype(f32)
                a_re, a_im = re_ref[block, rows, :], im_ref[block, rows, :]
                if delta == 0:
                    g_re = g_re + keep * (a_re * a_re + a_im * a_im)
                else:
                    b_re, b_im = re_ref[block + delta, rows, :], im_ref[block + delta, rows, :]
                    g_re = g_re + keep * (a_re * b_re + a_im * b_im)
                    g_im = g_im + keep * (a_im * b_re - a_re * b_im)
            for j in range(half):
                cosine, sine = waves_ref[j, wave_rows, :], waves_ref[half + j, wave_rows, :]
                sums[4 * j] = sums[4 * j] + cosine * g_re
                sums[4 * j + 1] = sums[4 * j + 1] + sine * g_re
                if delta > 0:
                    sums[4 * j + 2] = sums[4 * j + 2] + cosine * g_im
                    sums[4 * j + 3] = sums[4 * j + 3] + sine * g_im
        for n in range(4 * half):
            sums_ref[q, delta * 4 * half + n] = sums[n]


def to_offsets(blocks, q, sums_ref, h_ref, back_high_ref, back_low_ref, acc_ref):
    f32 = jnp.float32
    half = LAGS // 2
    chunk = sums_ref.shape[3]
    zero_row = (blocks - 1) * LAGS
    for delta in range(blocks):
        h_re, h_im = [None] * LAGS, [None] * LAGS
        for j in range(half):
            cr, sr, ci, si = [
                jnp.sum(sums_ref[q, (delta * half + j) * 4 + n], axis=0, keepdims=True) for n in range(4)
            ]
            h_re[half + j], h_im[half + j] = cr - si, ci + sr
            h_re[half - 1 - j], h_im[half - 1 - j] = cr + si, ci - sr
        ahead = zero_row + delta * LAGS
        h_ref[pl.ds(ahead, LAGS), pl.ds(0, chunk)] = jnp.concatenate(h_re, axis=0)
        h_ref[pl.ds(ahead, LAGS), pl.ds(chunk, chunk)] = jnp.concatenate(h_im, axis=0)
        if delta > 0:
            behind = zero_row - delta * LAGS
            h_ref[pl.ds(behind, LAGS), pl.ds(0, chunk)] = jnp.concatenate(h_re[::-1], axis=0)
            h_ref[pl.ds(behind, LAGS), pl.ds(chunk, chunk)] = -jnp.concatenate(h_im[::-1], axis=0)
    h_high, h_low = split_rounded(h_ref[...])
    count = h_ref.shape[0]
    both = jnp.dot(jnp.concatenate([h_high, h_low], axis=0), back_high_ref[q], preferred_element_type=f32)
    acc_ref[...] += both[:count] + both[count:] + jnp.dot(h_high, back_low_ref[q], preferred_element_type=f32)


def stack_kernel(
    blocks,
    mask_ref,
    taper_ref,
    waves_hbm,
    raw_hbm,
    table_hbm,
    high_hbm,
    low_hbm,
    back_high_hbm,
    back_low_hbm,
    out_ref,
    waves_ref,
    raw_ref,
    table_ref,
    high_ref,
    low_ref,
    back_high_ref,
    back_low_ref,
    cast_ref,
    series_ref,
    y_ref,
    spec_ref,
    pre_ref,
    suf_ref,
    all_ref,
    ready_ref,
    white_ref,
    lhs_ref,
    re_ref,
    im_ref,
    sums_ref,
    h_ref,
    acc_ref,
    part_ref,
    got_ref,
    plane_ref,
    plane_got_ref,
    raw_sem,
    table_sem,
    raw_send,
    raw_recv,
    white_send,
    white_recv,
    stack_send,
    stack_recv,
    plane_send,
    plane_recv,
):
    _, n_dev, rows, chans = series_ref.shape
    groups = n_dev // RADIX
    me = own_index()
    f32 = jnp.float32

    def raw_copy(chunk):
        part = pl.ds(pl.multiple_of(chunk * rows, rows), rows)
        return pltpu.make_async_copy(raw_hbm.at[part], raw_ref.at[part], raw_sem.at[chunk])

    def table_copy(n):
        pairs = (
            (table_hbm, table_ref),
            (high_hbm, high_ref),
            (low_hbm, low_ref),
            (back_high_hbm, back_high_ref),
            (back_low_hbm, back_low_ref),
            (waves_hbm.at[me], waves_ref),
        )
        src, dst = pairs[n]
        return pltpu.make_async_copy(src, dst, table_sem.at[n])

    n_tables = 6

    for chunk in range(RAW_CHUNKS):
        raw_copy(chunk).start()
    greet_all(n_dev)

    def send_raw(chunk):
        part = pl.ds(pl.multiple_of(chunk * rows, rows), rows)
        raw_copy(chunk).wait()
        for other in range(n_dev):
            cast_ref[chunk, other] = raw_ref[part, other * chans : (other + 1) * chans].astype(jnp.bfloat16)

    send_raw(0)
    meet_all(n_dev)
    start_all(n_dev, 0, cast_ref, series_ref, raw_send, raw_recv)

    send_raw(1)
    start_all(n_dev, 1, cast_ref, series_ref, raw_send, raw_recv)

    @pl.loop(2, RAW_CHUNKS)
    def _(chunk):
        send_raw(chunk)

    for n in range(n_tables):
        table_copy(n).start()
    spec_ref[...] = jnp.zeros_like(spec_ref)
    sums_ref[...] = jnp.zeros_like(sums_ref)
    acc_ref[...] = jnp.zeros_like(acc_ref)
    h_ref[...] = jnp.zeros_like(h_ref)
    table_copy(0).wait()

    @pl.loop(0, RAW_CHUNKS)
    def _(chunk):
        series_ref[chunk, me] = cast_ref[chunk, me]
        wait_sent(n_dev, chunk, cast_ref, series_ref, raw_send, raw_recv)

        @pl.when(chunk + 2 < RAW_CHUNKS)
        def _():
            start_all(n_dev, chunk + 2, cast_ref, series_ref, raw_send, raw_recv)

        wait_all(n_dev, chunk, cast_ref, series_ref, raw_send, raw_recv)
        transform(series_ref, chunk, y_ref, spec_ref, table_ref)

    window_sums(spec_ref, pre_ref, suf_ref, all_ref)
    bin_chunks = ready_ref.shape[0]
    per = bin_chunks * BIN_CHUNK

    @pl.loop(0, RADIX)
    def _(i):
        rho = (me // groups + 1 + i) % RADIX
        total = all_ref[...] + suf_ref[rho, pl.ds(PAD - 2, M_ROWS), :] + pre_ref[rho, pl.ds(PAD + 2, M_ROWS), :]
        scale = taper_ref[rho] / (total * (1.0 / (2 * SW + 1)) + EPS)
        for part in range(2):
            value = (spec_ref[rho, pl.ds(part * M_ROWS, M_ROWS), :] * scale).astype(jnp.bfloat16)
            for g in range(groups):
                for w in range(bin_chunks):
                    first = g * per + w * BIN_CHUNK
                    ready_ref[w, rho * groups + g, part] = value[first : first + BIN_CHUNK]
        for g in range(groups):
            other = rho * groups + g

            @pl.when(other != me)
            def _():
                slot_copy(ready_ref, white_ref, 0, other, me, white_send, white_recv, other).start()

    if bin_chunks > 1:
        start_all(n_dev, 1, ready_ref, white_ref, white_send, white_recv)

    for n in range(1, n_tables):
        table_copy(n).wait()
    per_block = n_dev // blocks
    q_chunks = sums_ref.shape[0]

    @pl.loop(0, bin_chunks)
    def _(w):
        white_ref[w, me] = ready_ref[w, me]
        wait_sent(n_dev, w, ready_ref, white_ref, white_send, white_recv)

        @pl.when(w + 2 < bin_chunks)
        def _():
            start_all(n_dev, w + 2, ready_ref, white_ref, white_send, white_recv)

        wait_all(n_dev, w, ready_ref, white_ref, white_send, white_recv)
        for source in range(n_dev):
            block, place = divmod(source, per_block)
            for part in range(2):
                lhs_ref[pl.ds((2 * block + part) * BIN_CHUNK, BIN_CHUNK), pl.ds(place * chans, chans)] = white_ref[
                    w, source, part
                ]

        @pl.loop(0, q_chunks)
        def _(q):
            cross_spectra(
                blocks, w, q, mask_ref, waves_ref, lhs_ref, high_ref, low_ref, re_ref, im_ref, sums_ref
            )

    @pl.loop(0, q_chunks)
    def _(q):
        to_offsets(blocks, q, sums_ref, h_ref, back_high_ref, back_low_ref, acc_ref)

    width = per_block * chans
    n_blk, n_lag, _, cols = part_ref.shape
    parts = width // cols
    for segment in range(2 * blocks):
        value = jnp.zeros((LAGS, width), f32)
        if segment < 2 * blocks - 1:
            value = value + acc_ref[pl.ds(segment * LAGS, LAGS), pl.ds(0, width)]
        if segment > 0:
            value = value + acc_ref[pl.ds((segment - 1) * LAGS, LAGS), pl.ds(width, width)]
        for part in range(parts):
            part_ref[*divmod(segment * parts + part, n_lag)] = value[:, part * cols : (part + 1) * cols]

    plane_ref[...] = sum_along("blk", part_ref, got_ref, stack_send, stack_recv)
    total = sum_along("lag", plane_ref, plane_got_ref, plane_send, plane_recv)
    columns = me * cols + lax.broadcasted_iota(jnp.int32, (LAGS, cols), 1)
    out_ref[...] = total * stack_scale(pair_counts(mask_ref, blocks, columns))


def stacked(raw, mask, n_dev):
    samples = raw.shape[0]
    chans = C // n_dev
    blocks = mask.shape[0]
    bins = NB // n_dev
    width = C // blocks
    size = 2 * width
    chunk = LANES
    cols = 2 * C // n_dev
    n_blk, n_lag = lax.axis_size("blk"), lax.axis_size("lag")
    waves = lag_waves(n_dev)
    bin_chunks = bins // BIN_CHUNK
    pairs = RADIX // 2
    f32, b16 = jnp.float32, jnp.bfloat16
    tables = [spectrum_tables(samples), *channel_tables(width, chunk), *offset_tables(width, chunk)]
    rows = 2 * blocks * LAGS
    whole = pl.BlockSpec(memory_space=pltpu.VMEM)
    away = pl.BlockSpec(memory_space=pl.ANY)
    return pl.pallas_call(
        functools.partial(stack_kernel, blocks),
        out_shape=jax.ShapeDtypeStruct((LAGS, cols), f32),
        in_specs=[pl.BlockSpec(memory_space=pltpu.SMEM), whole] + [away] * 7,
        out_specs=whole,
        scratch_shapes=[
            pltpu.VMEM(waves.shape[1:], f32),
            pltpu.VMEM(raw.shape, f32),
            *[pltpu.VMEM(table.shape, b16) for table in tables],
            pltpu.VMEM((RAW_CHUNKS, n_dev, samples // RAW_CHUNKS, chans), b16),
            pltpu.VMEM((RAW_CHUNKS, n_dev, samples // RAW_CHUNKS, chans), b16),
            pltpu.VMEM((pairs, 2 * SPAN // RAW_CHUNKS, chans), b16),
            pltpu.VMEM((RADIX, 2 * M_ROWS, chans), f32),
            pltpu.VMEM((RADIX, M_ROWS + 2 * PAD, chans), f32),
            pltpu.VMEM((RADIX, M_ROWS + 2 * PAD, chans), f32),
            pltpu.VMEM((M_ROWS, chans), f32),
            pltpu.VMEM((bin_chunks, n_dev, 2, BIN_CHUNK, chans), b16),
            pltpu.VMEM((bin_chunks, n_dev, 2, BIN_CHUNK, chans), b16),
            pltpu.VMEM((blocks * 2 * BIN_CHUNK, width), b16),
            pltpu.VMEM((blocks, BIN_CHUNK, chunk), f32),
            pltpu.VMEM((blocks, BIN_CHUNK, chunk), f32),
            pltpu.VMEM((size // chunk, blocks * 2 * LAGS, 8, chunk), f32),
            pltpu.VMEM((rows, 2 * chunk), f32),
            pltpu.VMEM((rows, size), f32),
            pltpu.VMEM((n_blk, n_lag, LAGS, cols), f32),
            pltpu.VMEM((n_blk, n_lag, LAGS, cols), f32),
            pltpu.VMEM((n_lag, LAGS, cols), f32),
            pltpu.VMEM((n_lag, LAGS, cols), f32),
            pltpu.SemaphoreType.DMA((RAW_CHUNKS,)),
            pltpu.SemaphoreType.DMA((len(tables) + 1,)),
            pltpu.SemaphoreType.DMA((RAW_CHUNKS, n_dev)),
            pltpu.SemaphoreType.DMA((RAW_CHUNKS, n_dev)),
            pltpu.SemaphoreType.DMA((bin_chunks, n_dev)),
            pltpu.SemaphoreType.DMA((bin_chunks, n_dev)),
            pltpu.SemaphoreType.DMA((n_blk,)),
            pltpu.SemaphoreType.DMA((n_blk,)),
            pltpu.SemaphoreType.DMA((n_lag,)),
            pltpu.SemaphoreType.DMA((n_lag,)),
        ],
        compiler_params=pltpu.CompilerParams(
            vmem_limit_bytes=58 * 2**20, collective_id=0, has_side_effects=True
        ),
        cost_estimate=pl.CostEstimate(flops=6 * 2**30, bytes_accessed=25 * 2**20, transcendentals=0),
        name="stacked",
    )(mask, jnp.asarray(taper_table()), jnp.asarray(waves), raw, *[jnp.asarray(table) for table in tables])


def pair_counts(mask_ref, blocks, columns):
    width = C // blocks
    offsets = columns - C
    counts = jnp.zeros_like(columns)
    for delta in range(1 - blocks, blocks):
        per_delta = sum(
            mask_ref[block, block + delta] for block in range(max(0, -delta), min(blocks, blocks - delta))
        )
        counts = counts + jnp.maximum(0, width - jnp.abs(offsets - width * delta)) * per_delta
    return counts


def stack_scale(counts):
    return 1.0 / jnp.sqrt(NB * jnp.maximum(counts, 1).astype(jnp.float32))


def on_device(raw, mask):
    n_dev = lax.axis_size("blk") * lax.axis_size("lag")
    return stacked(raw, mask, n_dev)


def solution(mesh):
    return jax.shard_map(
        on_device,
        mesh=mesh,
        in_specs=(P(("blk", "lag"), None), P()),
        out_specs=P(None, ("blk", "lag")),
        check_vma=False,
    )
```

```python
import functools
import math

import jax
import jax.numpy as jnp
import ml_dtypes
import numpy as np
from jax import lax
from jax.experimental import pallas as pl
from jax.experimental.pallas import tpu as pltpu
from jax.sharding import PartitionSpec as P

NT = 8192
C = 4096
NB = 2048
K0 = 16
SW = 32
TAPER = 128
LAGS = 8
LAG_STEP = 32
EPS = 1e-06

RADIX = 16
RAW_CHUNKS = 2
BIN_CHUNK = 16
SPAN = NT // RADIX
M_ROWS = NB // RADIX
LANES = 128
PAD = 8
bf16 = ml_dtypes.bfloat16


def split_high_low(table):
    high = table.astype(bf16)
    low = (table - high.astype(np.float64)).astype(bf16)
    return high, low


@functools.cache
def spectrum_tables(samples):
    m = np.arange(M_ROWS)[:, None] + 1
    s = np.arange(SPAN)[None, :]

    def waves(rho):
        angle = 2 * np.pi * (((RADIX * m + rho) * s) % NT) / NT
        return np.cos(angle), np.sin(angle)

    zero = np.zeros((M_ROWS, SPAN))
    tables = []
    c0, s0 = waves(0)
    c8, s8 = waves(RADIX // 2)
    tables.append(np.block([[c0, zero], [-s0, zero], [zero, c8], [zero, -s8]]))
    for rho in range(1, RADIX // 2):
        ca, sa = waves(rho)
        cb, sb = waves(RADIX - rho)
        tables.append(np.block([[ca, sa], [-sa, ca], [cb, -sb], [-sb, -cb]]))
    table = np.stack(tables).astype(bf16)
    rows = samples // RAW_CHUNKS
    shape = (RADIX // 2, 4 * M_ROWS, 2, SPAN // samples, RAW_CHUNKS, rows)
    table = table.reshape(shape).transpose(4, 0, 1, 2, 3, 5)
    return table.reshape(RAW_CHUNKS, RADIX // 2, 4 * M_ROWS, 2 * SPAN // RAW_CHUNKS)


@functools.cache
def taper_table():
    j = np.arange(NB, dtype=np.float64)
    edge = np.minimum(j, NB - 1 - j)
    weights = np.where(edge < TAPER, 0.5 - 0.5 * np.cos(math.pi * (edge + 0.5) / TAPER), 1.0)
    weights = weights.reshape(M_ROWS, RADIX).T
    return np.ascontiguousarray(weights.astype(np.float32)[:, :, None])


@functools.cache
def channel_tables(width, chunk):
    size = 2 * width
    c = np.arange(width)[:, None]
    q = np.arange(size)[None, :]
    angle = 2 * np.pi * ((c * q) % size) / size
    both = np.stack([np.cos(angle), np.sin(angle)], axis=1).reshape(width, 2, size // chunk, chunk)
    both = both.transpose(2, 0, 1, 3).reshape(size // chunk, width, 2 * chunk)
    return split_high_low(both)


@functools.cache
def offset_tables(width, chunk):
    size = 2 * width
    q = np.arange(size)[:, None]
    d = np.arange(size)[None, :] - width
    angle = 2 * np.pi * ((q * d) % size) / size
    both = np.stack([np.cos(angle), np.sin(angle)]) / size
    both[:, :, 0] = 0.0
    both = both.reshape(2, size // chunk, chunk, size).transpose(1, 0, 2, 3)
    return split_high_low(both.reshape(size // chunk, 2 * chunk, size))


@functools.cache
def lag_waves(n_dev):
    groups = n_dev // RADIX
    bins = NB // n_dev
    device = np.arange(n_dev)[:, None]
    k = RADIX * ((device % groups) * bins + np.arange(bins)[None, :] + 1) + device // groups
    number = np.arange(LAGS // 2) + LAGS // 2
    shifts = LAG_STEP * (2 * number + 1 - LAGS) // 2
    phase = 2 * np.pi * ((shifts[None, :, None] * k[:, None, :]) % NT) / NT
    waves = np.concatenate([np.cos(phase), np.sin(phase)], axis=1).astype(np.float32)
    return np.ascontiguousarray(np.broadcast_to(waves[..., None], (*waves.shape, LANES)))


def real_dft16(x):
    a = [x[h] + x[h + 8] for h in range(8)]
    b = [x[h] - x[h + 8] for h in range(8)]
    out = {}
    lo = [a[h] + a[h + 4] for h in range(4)]
    d = [a[h] - a[h + 4] for h in range(4)]
    out[0] = (lo[0] + lo[2]) + (lo[1] + lo[3])
    out[8] = (lo[0] + lo[2]) - (lo[1] + lo[3])
    out[4] = (lo[0] - lo[2], lo[3] - lo[1])
    root = math.sqrt(0.5)
    minus, plus = (d[1] - d[3]) * root, (d[1] + d[3]) * root
    out[2] = (d[0] + minus, -(d[2] + plus))
    out[6] = (d[0] - minus, d[2] - plus)
    diff = [None] + [b[h] - b[8 - h] for h in range(1, 4)]
    add = [None] + [b[h] + b[8 - h] for h in range(1, 4)]
    for rho in (1, 3, 5, 7):
        re, im = b[0], b[4] * (-math.sin(math.pi * rho / 2))
        for h in range(1, 4):
            re = re + diff[h] * math.cos(math.pi * h * rho / 8)
            im = im - add[h] * math.sin(math.pi * h * rho / 8)
        out[rho] = (re, im)
    return out


def own_index():
    return lax.axis_index("blk") * lax.axis_size("lag") + lax.axis_index("lag")


def coordinates(device):
    n_lag = lax.axis_size("lag")
    return (device // n_lag, device % n_lag)


def greet_all(n_dev):
    barrier = pltpu.get_barrier_semaphore()
    me = own_index()

    @pl.loop(1, n_dev)
    def _(ahead):
        other = (me + ahead) % n_dev
        pl.semaphore_signal(barrier, inc=1, device_id=coordinates(other), device_id_type=pl.DeviceIdType.MESH)


def meet_all(n_dev):
    pl.semaphore_wait(pltpu.get_barrier_semaphore(), n_dev - 1)


def split_rounded(value):
    high = value.astype(jnp.bfloat16)
    return high, (value - high.astype(jnp.float32)).astype(jnp.bfloat16)


def slot_copy(src_ref, dst_ref, chunk, src, dst, send_sem, recv_sem, device):
    return pltpu.make_async_remote_copy(
        src_ref=src_ref.at[chunk, src],
        dst_ref=dst_ref.at[chunk, dst],
        send_sem=send_sem.at[chunk, src],
        recv_sem=recv_sem.at[chunk, dst],
        device_id=coordinates(device),
        device_id_type=pl.DeviceIdType.MESH,
    )


def start_all(n_dev, chunk, src_ref, dst_ref, send_sem, recv_sem):
    me = own_index()

    @pl.loop(1, n_dev)
    def _(ahead):
        other = (me + ahead) % n_dev
        slot_copy(src_ref, dst_ref, chunk, other, me, send_sem, recv_sem, other).start()


def wait_all(n_dev, chunk, src_ref, dst_ref, send_sem, recv_sem):
    me = own_index()

    @pl.loop(1, n_dev)
    def _(ahead):
        other = (me + ahead) % n_dev
        slot_copy(src_ref, dst_ref, chunk, other, other, send_sem, recv_sem, other).wait_recv()


def wait_sent(n_dev, chunk, src_ref, dst_ref, send_sem, recv_sem):
    me = own_index()

    @pl.loop(1, n_dev)
    def _(ahead):
        other = (me + ahead) % n_dev
        slot_copy(src_ref, dst_ref, chunk, other, other, send_sem, recv_sem, other).wait_send()


def sum_along(axis, src_ref, got_ref, send_sem, recv_sem):
    size = lax.axis_size(axis)
    me = lax.axis_index(axis)

    def copy(src, dst, device):
        return pltpu.make_async_remote_copy(
            src_ref=src_ref.at[src],
            dst_ref=got_ref.at[dst],
            send_sem=send_sem.at[src],
            recv_sem=recv_sem.at[dst],
            device_id={axis: device},
            device_id_type=pl.DeviceIdType.MESH,
        )

    @pl.loop(1, size)
    def _(ahead):
        other = (me + ahead) % size
        copy(other, me, other).start()

    got_ref[me] = src_ref[me]

    @pl.loop(1, size)
    def _(ahead):
        other = (me + ahead) % size
        copy(other, other, other).wait_recv()

    @pl.loop(1, size)
    def _(ahead):
        other = (me + ahead) % size
        copy(other, other, other).wait_send()

    return jnp.sum(got_ref[...], axis=0)


def transform(series_ref, chunk, y_ref, spec_ref, table_ref):
    half = RADIX // 2
    tile = 16
    _, n_dev, rows, _ = series_ref.shape
    pieces = n_dev // RADIX
    span = pieces * rows
    per_piece = rows // tile

    @pl.loop(0, span // tile)
    def _(i):
        start = pl.multiple_of(i * tile, tile)
        inside = pl.multiple_of((i % per_piece) * tile, tile)
        x = [
            series_ref[chunk, h * pieces + i // per_piece, pl.ds(inside, tile), :].astype(jnp.float32)
            for h in range(RADIX)
        ]
        y = real_dft16(x)
        y[0] = (y[0], y[half])
        for rho in range(half):
            for part in range(2):
                y_ref[rho, pl.ds(part * span + start, tile), :] = y[rho][part].astype(jnp.bfloat16)

    @pl.loop(0, half)
    def _(pair):
        both = jnp.dot(table_ref[chunk, pair], y_ref[pair], preferred_element_type=jnp.float32)
        other = jnp.where(pair == 0, half, RADIX - pair)
        spec_ref[pair] += both[: 2 * M_ROWS]
        spec_ref[other] += both[2 * M_ROWS :]


def window_sums(spec_ref, pre_ref, suf_ref, all_ref):
    edge = jnp.zeros((PAD, all_ref.shape[1]), jnp.float32)
    inner = pl.ds(PAD, M_ROWS)
    for rho in range(RADIX):
        re = spec_ref[rho, pl.ds(0, M_ROWS), :]
        im = spec_ref[rho, pl.ds(M_ROWS, M_ROWS), :]
        amp = jnp.sqrt(re * re + im * im)
        suf_ref[rho, inner, :] = amp
        pre_ref[rho, inner, :] = amp if rho == 0 else pre_ref[rho - 1, inner, :] + amp
        for ref in (pre_ref, suf_ref):
            ref[rho, pl.ds(0, PAD), :] = edge
            ref[rho, pl.ds(PAD + M_ROWS, PAD), :] = edge
    for rho in range(RADIX - 2, -1, -1):
        suf_ref[rho, inner, :] = suf_ref[rho, inner, :] + suf_ref[rho + 1, inner, :]
    last = RADIX - 1
    all_ref[...] = (
        pre_ref[last, pl.ds(PAD - 1, M_ROWS), :]
        + pre_ref[last, inner, :]
        + pre_ref[last, pl.ds(PAD + 1, M_ROWS), :]
    )


def cross_spectra(blocks, bin_chunk, q, mask_ref, waves_ref, lhs_ref, high_ref, low_ref, re_ref, im_ref, sums_ref):
    f32 = jnp.float32
    half = LAGS // 2
    chunk = re_ref.shape[2]
    bins = BIN_CHUNK
    lhs = lhs_ref[...]
    product = jnp.dot(lhs, high_ref[q], preferred_element_type=f32)
    product = product + jnp.dot(lhs, low_ref[q], preferred_element_type=f32)
    for block in range(blocks):
        real = product[2 * block * bins : (2 * block + 1) * bins]
        imag = product[(2 * block + 1) * bins : (2 * block + 2) * bins]
        re_ref[block] = real[:, :chunk] + imag[:, chunk:]
        im_ref[block] = imag[:, :chunk] - real[:, chunk:]
    for delta in range(blocks):
        sums = [sums_ref[q, delta * 4 * half + n] for n in range(4 * half)]
        for b in range(bins // 8):
            rows = pl.ds(8 * b, 8)
            wave_rows = pl.ds(pl.multiple_of(bin_chunk * bins + 8 * b, 8), 8)
            g_re = jnp.zeros((8, chunk), f32)
            g_im = jnp.zeros((8, chunk), f32)
            for block in range(blocks - delta):
                keep = mask_ref[block, block + delta].astype(f32)
                a_re, a_im = re_ref[block, rows, :], im_ref[block, rows, :]
                if delta == 0:
                    g_re = g_re + keep * (a_re * a_re + a_im * a_im)
                else:
                    b_re, b_im = re_ref[block + delta, rows, :], im_ref[block + delta, rows, :]
                    g_re = g_re + keep * (a_re * b_re + a_im * b_im)
                    g_im = g_im + keep * (a_im * b_re - a_re * b_im)
            for j in range(half):
                cosine, sine = waves_ref[j, wave_rows, :], waves_ref[half + j, wave_rows, :]
                sums[4 * j] = sums[4 * j] + cosine * g_re
                sums[4 * j + 1] = sums[4 * j + 1] + sine * g_re
                if delta > 0:
                    sums[4 * j + 2] = sums[4 * j + 2] + cosine * g_im
                    sums[4 * j + 3] = sums[4 * j + 3] + sine * g_im
        for n in range(4 * half):
            sums_ref[q, delta * 4 * half + n] = sums[n]


def to_offsets(blocks, q, sums_ref, h_ref, back_high_ref, back_low_ref, acc_ref):
    f32 = jnp.float32
    half = LAGS // 2
    chunk = sums_ref.shape[3]
    zero_row = (blocks - 1) * LAGS
    for delta in range(blocks):
        h_re, h_im = [None] * LAGS, [None] * LAGS
        for j in range(half):
            cr, sr, ci, si = [
                jnp.sum(sums_ref[q, (delta * half + j) * 4 + n], axis=0, keepdims=True) for n in range(4)
            ]
            h_re[half + j], h_im[half + j] = cr - si, ci + sr
            h_re[half - 1 - j], h_im[half - 1 - j] = cr + si, ci - sr
        ahead = zero_row + delta * LAGS
        h_ref[pl.ds(ahead, LAGS), pl.ds(0, chunk)] = jnp.concatenate(h_re, axis=0)
        h_ref[pl.ds(ahead, LAGS), pl.ds(chunk, chunk)] = jnp.concatenate(h_im, axis=0)
        if delta > 0:
            behind = zero_row - delta * LAGS
            h_ref[pl.ds(behind, LAGS), pl.ds(0, chunk)] = jnp.concatenate(h_re[::-1], axis=0)
            h_ref[pl.ds(behind, LAGS), pl.ds(chunk, chunk)] = -jnp.concatenate(h_im[::-1], axis=0)
    h_high, h_low = split_rounded(h_ref[...])
    count = h_ref.shape[0]
    both = jnp.dot(jnp.concatenate([h_high, h_low], axis=0), back_high_ref[q], preferred_element_type=f32)
    acc_ref[...] += both[:count] + both[count:] + jnp.dot(h_high, back_low_ref[q], preferred_element_type=f32)


def stack_kernel(
    blocks,
    mask_ref,
    taper_ref,
    waves_hbm,
    raw_hbm,
    table_hbm,
    high_hbm,
    low_hbm,
    back_high_hbm,
    back_low_hbm,
    out_ref,
    waves_ref,
    raw_ref,
    table_ref,
    high_ref,
    low_ref,
    back_high_ref,
    back_low_ref,
    cast_ref,
    series_ref,
    y_ref,
    spec_ref,
    pre_ref,
    suf_ref,
    all_ref,
    ready_ref,
    white_ref,
    lhs_ref,
    re_ref,
    im_ref,
    sums_ref,
    h_ref,
    acc_ref,
    part_ref,
    got_ref,
    plane_ref,
    plane_got_ref,
    raw_sem,
    table_sem,
    raw_send,
    raw_recv,
    white_send,
    white_recv,
    stack_send,
    stack_recv,
    plane_send,
    plane_recv,
):
    _, n_dev, rows, chans = series_ref.shape
    groups = n_dev // RADIX
    me = own_index()
    f32 = jnp.float32

    def raw_copy(chunk):
        part = pl.ds(pl.multiple_of(chunk * rows, rows), rows)
        return pltpu.make_async_copy(raw_hbm.at[part], raw_ref.at[part], raw_sem.at[chunk])

    def table_copy(n):
        pairs = (
            (table_hbm, table_ref),
            (high_hbm, high_ref),
            (low_hbm, low_ref),
            (back_high_hbm, back_high_ref),
            (back_low_hbm, back_low_ref),
            (waves_hbm.at[me], waves_ref),
        )
        src, dst = pairs[n]
        return pltpu.make_async_copy(src, dst, table_sem.at[n])

    n_tables = 6

    for chunk in range(RAW_CHUNKS):
        raw_copy(chunk).start()
    greet_all(n_dev)

    def send_raw(chunk):
        part = pl.ds(pl.multiple_of(chunk * rows, rows), rows)
        raw_copy(chunk).wait()
        for other in range(n_dev):
            cast_ref[chunk, other] = raw_ref[part, other * chans : (other + 1) * chans].astype(jnp.bfloat16)

    send_raw(0)
    meet_all(n_dev)
    start_all(n_dev, 0, cast_ref, series_ref, raw_send, raw_recv)

    send_raw(1)
    start_all(n_dev, 1, cast_ref, series_ref, raw_send, raw_recv)

    @pl.loop(2, RAW_CHUNKS)
    def _(chunk):
        send_raw(chunk)

    for n in range(n_tables):
        table_copy(n).start()
    spec_ref[...] = jnp.zeros_like(spec_ref)
    sums_ref[...] = jnp.zeros_like(sums_ref)
    acc_ref[...] = jnp.zeros_like(acc_ref)
    h_ref[...] = jnp.zeros_like(h_ref)
    table_copy(0).wait()

    @pl.loop(0, RAW_CHUNKS)
    def _(chunk):
        series_ref[chunk, me] = cast_ref[chunk, me]
        wait_sent(n_dev, chunk, cast_ref, series_ref, raw_send, raw_recv)

        @pl.when(chunk + 2 < RAW_CHUNKS)
        def _():
            start_all(n_dev, chunk + 2, cast_ref, series_ref, raw_send, raw_recv)

        wait_all(n_dev, chunk, cast_ref, series_ref, raw_send, raw_recv)
        transform(series_ref, chunk, y_ref, spec_ref, table_ref)

    window_sums(spec_ref, pre_ref, suf_ref, all_ref)
    bin_chunks = ready_ref.shape[0]
    per = bin_chunks * BIN_CHUNK

    @pl.loop(0, RADIX)
    def _(i):
        rho = (me // groups + 1 + i) % RADIX
        total = all_ref[...] + suf_ref[rho, pl.ds(PAD - 2, M_ROWS), :] + pre_ref[rho, pl.ds(PAD + 2, M_ROWS), :]
        scale = taper_ref[rho] / (total * (1.0 / (2 * SW + 1)) + EPS)
        for part in range(2):
            value = (spec_ref[rho, pl.ds(part * M_ROWS, M_ROWS), :] * scale).astype(jnp.bfloat16)
            for g in range(groups):
                for w in range(bin_chunks):
                    first = g * per + w * BIN_CHUNK
                    ready_ref[w, rho * groups + g, part] = value[first : first + BIN_CHUNK]
        for g in range(groups):
            other = rho * groups + g

            @pl.when(other != me)
            def _():
                slot_copy(ready_ref, white_ref, 0, other, me, white_send, white_recv, other).start()

    if bin_chunks > 1:
        start_all(n_dev, 1, ready_ref, white_ref, white_send, white_recv)

    for n in range(1, n_tables):
        table_copy(n).wait()
    per_block = n_dev // blocks
    q_chunks = sums_ref.shape[0]

    @pl.loop(0, bin_chunks)
    def _(w):
        white_ref[w, me] = ready_ref[w, me]
        wait_sent(n_dev, w, ready_ref, white_ref, white_send, white_recv)

        @pl.when(w + 2 < bin_chunks)
        def _():
            start_all(n_dev, w + 2, ready_ref, white_ref, white_send, white_recv)

        wait_all(n_dev, w, ready_ref, white_ref, white_send, white_recv)
        for source in range(n_dev):
            block, place = divmod(source, per_block)
            for part in range(2):
                lhs_ref[pl.ds((2 * block + part) * BIN_CHUNK, BIN_CHUNK), pl.ds(place * chans, chans)] = white_ref[
                    w, source, part
                ]

        @pl.loop(0, q_chunks)
        def _(q):
            cross_spectra(
                blocks, w, q, mask_ref, waves_ref, lhs_ref, high_ref, low_ref, re_ref, im_ref, sums_ref
            )

    @pl.loop(0, q_chunks)
    def _(q):
        to_offsets(blocks, q, sums_ref, h_ref, back_high_ref, back_low_ref, acc_ref)

    width = per_block * chans
    n_blk, n_lag, _, cols = part_ref.shape
    parts = width // cols
    for segment in range(2 * blocks):
        value = jnp.zeros((LAGS, width), f32)
        if segment < 2 * blocks - 1:
            value = value + acc_ref[pl.ds(segment * LAGS, LAGS), pl.ds(0, width)]
        if segment > 0:
            value = value + acc_ref[pl.ds((segment - 1) * LAGS, LAGS), pl.ds(width, width)]
        for part in range(parts):
            part_ref[*divmod(segment * parts + part, n_lag)] = value[:, part * cols : (part + 1) * cols]

    plane_ref[...] = sum_along("blk", part_ref, got_ref, stack_send, stack_recv)
    total = sum_along("lag", plane_ref, plane_got_ref, plane_send, plane_recv)
    columns = me * cols + lax.broadcasted_iota(jnp.int32, (LAGS, cols), 1)
    out_ref[...] = total * stack_scale(pair_counts(mask_ref, blocks, columns))


def stacked(raw, mask, n_dev):
    samples = raw.shape[0]
    chans = C // n_dev
    blocks = mask.shape[0]
    bins = NB // n_dev
    width = C // blocks
    size = 2 * width
    chunk = LANES
    cols = 2 * C // n_dev
    n_blk, n_lag = lax.axis_size("blk"), lax.axis_size("lag")
    waves = lag_waves(n_dev)
    bin_chunks = bins // BIN_CHUNK
    pairs = RADIX // 2
    f32, b16 = jnp.float32, jnp.bfloat16
    tables = [spectrum_tables(samples), *channel_tables(width, chunk), *offset_tables(width, chunk)]
    rows = 2 * blocks * LAGS
    whole = pl.BlockSpec(memory_space=pltpu.VMEM)
    away = pl.BlockSpec(memory_space=pl.ANY)
    return pl.pallas_call(
        functools.partial(stack_kernel, blocks),
        out_shape=jax.ShapeDtypeStruct((LAGS, cols), f32),
        in_specs=[pl.BlockSpec(memory_space=pltpu.SMEM), whole] + [away] * 7,
        out_specs=whole,
        scratch_shapes=[
            pltpu.VMEM(waves.shape[1:], f32),
            pltpu.VMEM(raw.shape, f32),
            *[pltpu.VMEM(table.shape, b16) for table in tables],
            pltpu.VMEM((RAW_CHUNKS, n_dev, samples // RAW_CHUNKS, chans), b16),
            pltpu.VMEM((RAW_CHUNKS, n_dev, samples // RAW_CHUNKS, chans), b16),
            pltpu.VMEM((pairs, 2 * SPAN // RAW_CHUNKS, chans), b16),
            pltpu.VMEM((RADIX, 2 * M_ROWS, chans), f32),
            pltpu.VMEM((RADIX, M_ROWS + 2 * PAD, chans), f32),
            pltpu.VMEM((RADIX, M_ROWS + 2 * PAD, chans), f32),
            pltpu.VMEM((M_ROWS, chans), f32),
            pltpu.VMEM((bin_chunks, n_dev, 2, BIN_CHUNK, chans), b16),
            pltpu.VMEM((bin_chunks, n_dev, 2, BIN_CHUNK, chans), b16),
            pltpu.VMEM((blocks * 2 * BIN_CHUNK, width), b16),
            pltpu.VMEM((blocks, BIN_CHUNK, chunk), f32),
            pltpu.VMEM((blocks, BIN_CHUNK, chunk), f32),
            pltpu.VMEM((size // chunk, blocks * 2 * LAGS, 8, chunk), f32),
            pltpu.VMEM((rows, 2 * chunk), f32),
            pltpu.VMEM((rows, size), f32),
            pltpu.VMEM((n_blk, n_lag, LAGS, cols), f32),
            pltpu.VMEM((n_blk, n_lag, LAGS, cols), f32),
            pltpu.VMEM((n_lag, LAGS, cols), f32),
            pltpu.VMEM((n_lag, LAGS, cols), f32),
            pltpu.SemaphoreType.DMA((RAW_CHUNKS,)),
            pltpu.SemaphoreType.DMA((len(tables) + 1,)),
            pltpu.SemaphoreType.DMA((RAW_CHUNKS, n_dev)),
            pltpu.SemaphoreType.DMA((RAW_CHUNKS, n_dev)),
            pltpu.SemaphoreType.DMA((bin_chunks, n_dev)),
            pltpu.SemaphoreType.DMA((bin_chunks, n_dev)),
            pltpu.SemaphoreType.DMA((n_blk,)),
            pltpu.SemaphoreType.DMA((n_blk,)),
            pltpu.SemaphoreType.DMA((n_lag,)),
            pltpu.SemaphoreType.DMA((n_lag,)),
        ],
        compiler_params=pltpu.CompilerParams(
            vmem_limit_bytes=58 * 2**20, collective_id=0, has_side_effects=True
        ),
        cost_estimate=pl.CostEstimate(flops=6 * 2**30, bytes_accessed=25 * 2**20, transcendentals=0),
        name="stacked",
    )(mask, jnp.asarray(taper_table()), jnp.asarray(waves), raw, *[jnp.asarray(table) for table in tables])


def pair_counts(mask_ref, blocks, columns):
    width = C // blocks
    offsets = columns - C
    counts = jnp.zeros_like(columns)
    for delta in range(1 - blocks, blocks):
        per_delta = sum(
            mask_ref[block, block + delta] for block in range(max(0, -delta), min(blocks, blocks - delta))
        )
        counts = counts + jnp.maximum(0, width - jnp.abs(offsets - width * delta)) * per_delta
    return counts


def stack_scale(counts):
    return 1.0 / jnp.sqrt(NB * jnp.maximum(counts, 1).astype(jnp.float32))


def on_device(raw, mask):
    n_dev = lax.axis_size("blk") * lax.axis_size("lag")
    return stacked(raw, mask, n_dev)


def solution(mesh):
    return jax.shard_map(
        on_device,
        mesh=mesh,
        in_specs=(P(("blk", "lag"), None), P()),
        out_specs=P(None, ("blk", "lag")),
        check_vma=False,
    )
```
